512 devices in a mesh: region: 32 (over x, z_lo), run: 16 (over z_hi, y, core).
Axes of the slice: x: 4, y: 4, z: 16 (z_hi: 2, z_lo: 8; z = z_hi * 8 + z_lo), core: 2. Of those that a mesh axis runs over, the one named last changes fastest.
Arguments:
- sensitivity: bfloat16 [12288, 65536], P('run', 'region'), may hold values from -0.75 to 0.75
- run_counts: int32 [512], P('region'), may hold values from 768 to 3072
- req_owner: int32 [1024, 1], P('region'), may hold values from 0 to 31; in each aligned block of 32 rows (0 to 31, 32 to 63, ...) no two rows name the same one
- req_block: int32 [1024], P('region'), may hold values from 0 to 15
- coupled: int32 [1024, 2], P('region'), may hold values from 0 to 15, all different within a row
Outputs:
- fisher: bfloat16 [1024, 2, 128, 128], P('region', None, 'run')
- mirror: bfloat16 [32, 32, 1, 2, 128, 128], P('region', None, None, None, None, 'run')
The draws below stay inside these ranges and needn't reach their ends.
Inputs may be any that keep to these rules, and one draw needn't show every extreme that they name: `req_owner`: among the requests of one region device every owner is named exactly 1 times. `coupled`: the 2 local blocks of one request differ.
All inputs are finite; a program needn't handle non-finite values.
Results may differ from the reference program's by a relative error of at most 0.001.
Values may be sent and summed in bfloat16 or wider, within the bound.
A program may use at most 128 MiB of HBM per device.

```python
import math
import jax
import jax.numpy as jnp
import numpy as np
from jax import lax

BS = 128
BLK_DEV = 16
OBS = 4
COUPLE = 2
CAP = 1
RUNS = 3072
ROWS = 12288
NBLK = 512
PARAMS = 65536
REQ_DEV = 32
NREQ = 1024
N_REGION = 32
N_RUN = 16


def place_ends(drawn, rng, low, largest):
    spot = [jax.random.randint(jax.random.fold_in(rng, axis), (), 0, length) for axis, length in enumerate(drawn.shape)]
    main_axis = drawn.shape.index(max(drawn.shape))
    next_to = spot[:main_axis] + [(spot[main_axis] + 1) % drawn.shape[main_axis]] + spot[main_axis + 1:]
    return drawn.at[tuple(spot)].set(low).at[tuple(next_to)].set(largest)


def shard_levels(own_key, extent, shards, least, high):
    level = 1.0
    for dim, shards_of in shards:
        draws = jax.random.uniform(jax.random.fold_in(jax.random.fold_in(own_key, 6), dim), (shards_of,), jnp.float32, least / len(shards), high / len(shards))
        level = level * jnp.repeat(jnp.exp(draws), extent[dim] // shards_of).reshape((-1,) + (1,) * (len(extent) - 1 - dim))
    return level


def distinct(stream_key, rows, amount, top, lift):
    order = jax.random.permutation(jax.random.fold_in(stream_key, 1), amount)
    boost = order
    for power in range(3):
        boost = boost * boost // amount
    boost = boost * lift // amount
    tickets = jax.random.randint(jax.random.fold_in(stream_key, 2), (rows, amount), 0, 4096) + boost
    sure = jax.random.permutation(jax.random.fold_in(stream_key, 3), rows)[jnp.arange(amount) % rows]
    tickets = jnp.where(jnp.arange(rows)[:, None] == sure[None, :], 1 << 14, tickets)
    score = tickets * amount + jnp.arange(amount)
    return lax.top_k(score.astype(jnp.int32), top)[1].astype(jnp.int32)


def deal_out(own_key, own, number, rows, amount, top, most, lean):
    ranking = jax.random.permutation(own_key, amount)
    crowded, ordinary = portions_of(amount, rows * top, most, lean, True), portions_of(amount, rows * top, most, lean, False)
    places = jnp.arange(amount)

    def named(tallies, rotation):
        used = int((tallies > 0).sum())
        fixed = max(1, used // 4)
        shifted = fixed + (places - fixed + rotation * (used - fixed)) % max(1, amount - fixed)
        return jnp.zeros((amount,), jnp.int32).at[ranking[jnp.where(places < fixed, places, shifted)]].set(jnp.asarray(tallies, jnp.int32))

    tallies = jnp.where(number % 4 == 0, named(crowded, number // 4), named(ordinary, number - number // 4 - 1))
    mixed = jax.random.permutation(jax.random.fold_in(own, 3), amount)
    source_of, taker = mixed[0:amount // 2 * 2:2], mixed[1:amount // 2 * 2:2]
    margin = jnp.minimum(tallies[source_of] - 1, most - tallies[taker]) // 2
    margin = jnp.where((source_of == ranking[0]) | (taker == ranking[0]) | (tallies[taker] == 0), 0, jnp.maximum(margin, 0))
    shifted = jax.random.randint(jax.random.fold_in(own, 4), (amount // 2,), 0, 1 << 20) % (margin + 1)
    tallies = tallies.at[source_of].add(-shifted).at[taker].add(shifted)
    items = jnp.searchsorted(jnp.cumsum(tallies), jnp.arange(rows * top), side="right").astype(jnp.int32)
    listing = items.reshape(top, rows).T
    listing = listing[jax.random.permutation(jax.random.fold_in(own, 1), rows)]
    rotation = jax.random.randint(jax.random.fold_in(own, 2), (rows, 1), 0, top)
    return jnp.take_along_axis(listing, (jnp.arange(top)[None, :] + rotation) % top, axis=1)


def portions_of(number_of, total, reach, lean, full):
    loads = [(1 << 20) // math.isqrt(standing ** lean) + 1 for standing in range(1, number_of + 1)]
    largest = reach if full else min(reach, max(-(-total // number_of), total * loads[0] // sum(loads)))
    least = 1 if total - largest >= number_of - 1 else 0
    holding, surplus = [largest] + [least] * (number_of - 1), total - largest - least * (number_of - 1)
    while surplus > 0:
        movable = [i for i in range(1, number_of) if holding[i] < largest] or [i for i in range(1, number_of) if holding[i] < reach]
        mass, left = sum([loads[i] for i in movable]), surplus
        for i in movable:
            extra = min(reach - holding[i], max(1, left * loads[i] // mass), surplus)
            holding[i] = holding[i] + extra
            surplus = surplus - extra
    return np.array(holding)


def normal_values(stream_key, extent, width, bound, split=(), kind=jnp.bfloat16):
    array = width * jax.random.normal(stream_key, extent, jnp.float32)
    if split:
        array = array * shard_levels(stream_key, extent, split, -0.22, 0.18)
    return jnp.clip(array, -bound, bound).astype(kind)


def setup_inputs(seed: int = 0) -> dict:
    seeds = jax.random.split(jax.random.key(seed), 6)
    sensitivity = normal_values(seeds[0], (ROWS, PARAMS), 0.125, 0.75, ((0, 16), (1, 32)))
    run_counts = place_ends(jax.random.randint(seeds[1], (NBLK,), RUNS // 4, RUNS + 1), jax.random.fold_in(seeds[1], 1), RUNS // 4, RUNS).astype(jnp.int32)
    req_owner_keys = jax.random.split(jax.random.fold_in(seeds[2], 1), NREQ // REQ_DEV)
    req_owner_turns = jax.random.permutation(jax.random.fold_in(seeds[2], 3), NREQ // REQ_DEV)
    req_owner = jax.vmap(lambda own, number: deal_out(jax.random.fold_in(seeds[2], 2), own, number, REQ_DEV, N_REGION, 1, CAP, 0))(req_owner_keys, req_owner_turns).reshape((NREQ, 1))
    req_block = place_ends(jax.random.randint(seeds[3], (NREQ,), 0, BLK_DEV), jax.random.fold_in(seeds[3], 1), 0, BLK_DEV - 1).astype(jnp.int32)
    coupled = distinct(seeds[4], NREQ, BLK_DEV, COUPLE, 0)
    return {"sensitivity": sensitivity, "run_counts": run_counts, "req_owner": req_owner, "req_block": req_block, "coupled": coupled}


def reference(sensitivity, run_counts, req_owner, req_block, coupled):
    row_run = jnp.arange(ROWS, dtype=jnp.int32) // OBS
    owner_of = req_owner[:, 0]
    width_range = jnp.arange(BS, dtype=jnp.int32)

    def one_request(request):
        region = request // REQ_DEV
        far_block = (owner_of[request] * BLK_DEV + req_block[request]).astype(jnp.int32)
        remote = lax.dynamic_slice_in_dim(sensitivity, (far_block * BS).astype(jnp.int32), BS, 1)
        remote = jnp.where((row_run < run_counts[far_block])[:, None], remote, jnp.zeros((), jnp.bfloat16))
        near_blocks = (region * BLK_DEV + coupled[request]).astype(jnp.int32)
        near_cols = (near_blocks[:, None] * BS + width_range[None, :]).reshape(-1)
        near = jnp.take(sensitivity, near_cols, axis=1)
        near_live = row_run[:, None] < jnp.repeat(run_counts[near_blocks], BS)[None, :]
        near = jnp.where(near_live, near, jnp.zeros((), jnp.bfloat16))
        near_f = near.astype(jnp.float32).reshape(N_RUN, ROWS // N_RUN, COUPLE * BS)
        far_f = remote.astype(jnp.float32).reshape(N_RUN, ROWS // N_RUN, BS)
        partials = jnp.einsum("trm,trn->tmn", near_f, far_f)
        total = jnp.sum(partials, axis=0).astype(jnp.bfloat16)
        return total.reshape(COUPLE, BS, BS)

    fisher = lax.map(one_request, jnp.arange(NREQ, dtype=jnp.int32))
    owner_grid = owner_of.reshape(N_REGION, REQ_DEV)
    ordinal = jnp.arange(REQ_DEV, dtype=jnp.int32)
    earlier = (owner_grid[:, :, None] == owner_grid[:, None, :]) & (ordinal[None, None, :] < ordinal[None, :, None])
    position = jnp.sum(earlier.astype(jnp.int32), axis=2).reshape(-1)
    source = jnp.arange(NREQ, dtype=jnp.int32) // REQ_DEV
    mirror = jnp.zeros((N_REGION, N_REGION, CAP, COUPLE, BS, BS), jnp.bfloat16)
    mirror = mirror.at[owner_of, source, position].set(jnp.swapaxes(fisher, 2, 3))
    return fisher, mirror
```

```python
import jax
import jax.numpy as jnp
from jax import lax
from jax.sharding import Mesh, PartitionSpec as P

OBS = 4
COUPLE = 2
BS = 128
PLANE = ("x", "y", "core")
REGION = ("x", "zlo")
RUN = ("zhi", "y", "core")


def shards(sensitivity, run_counts, req_owner, req_block, coupled):
    rows_dev = sensitivity.shape[0]
    blocks = run_counts.shape[0]
    requests = req_owner.shape[0]
    regions = lax.axis_size(REGION)
    zlo = lax.axis_size("zlo")
    runs = lax.axis_size(RUN)
    chunk = rows_dev // zlo
    mine = lax.axis_index(PLANE)

    table = jnp.concatenate([req_owner, req_block[:, None], coupled], axis=1)
    tables = lax.all_gather(table, REGION, axis=0, tiled=False)

    first_run = lax.axis_index(RUN) * (rows_dev // OBS)
    row_run = first_run + jnp.arange(rows_dev, dtype=jnp.int32) // OBS
    counts = jnp.repeat(run_counts, BS)
    masked = jnp.where(row_run[:, None] < counts[None, :], sensitivity, jnp.zeros((), jnp.bfloat16))
    part = lax.all_to_all(masked.reshape(zlo, chunk, blocks * BS), "zlo", 0, 0, tiled=True)
    part = lax.all_to_all(part, ("y", "core"), 0, 0, tiled=True)
    local = part.reshape(rows_dev, blocks, BS)

    asked = jnp.sum(jnp.where(tables[:, :, 0] == mine, tables[:, :, 1], 0), axis=1)
    outgoing = jnp.transpose(jnp.take(local, asked, axis=1), (1, 0, 2))
    arrived = lax.all_to_all(outgoing, PLANE, 0, 0, tiled=True)

    own = lax.dynamic_index_in_dim(tables, mine, 0, keepdims=False)
    hit = own[:, 0][None, :] == jnp.arange(regions, dtype=jnp.int32)[:, None]
    near = jnp.sum(jnp.where(hit[:, :, None], own[None, :, 2:], 0), axis=1)
    local_cols = jnp.take(local, near.reshape(-1), axis=1).reshape(rows_dev, regions, COUPLE, BS)
    partial_value = jnp.einsum(
        "rkcm,krn->mkcn", local_cols, arrived, preferred_element_type=jnp.float32
    )
    summed = lax.psum_scatter(partial_value, ("zhi", "zlo"), scatter_dimension=0, tiled=True)
    held = summed.astype(jnp.bfloat16)

    ny = lax.axis_size("y")
    nc = lax.axis_size("core")
    pairs = []
    for a in range(zlo):
        for y in range(ny):
            for c in range(nc):
                pairs.append(((a * ny + y) * nc + c, ((y * nc + c) * ny + a // nc) * nc + a % nc))
    slices = lax.ppermute(held, ("zlo", "y", "core"), pairs)
    mslice = slices.shape[0]
    by_owner = jnp.transpose(slices, (1, 2, 0, 3))
    fisher = jnp.take(by_owner, req_owner[:, 0], axis=0)
    placed = jnp.transpose(slices, (1, 2, 3, 0))
    returned = lax.all_to_all(placed, REGION, 0, 0, tiled=True)
    return fisher, returned.reshape(1, regions, 1, COUPLE, BS, mslice)


def solution(mesh):
    fine = Mesh(mesh.devices.reshape(4, 8, 2, 4, 2), ("x", "zlo", "zhi", "y", "core"))
    in_specs = (P(RUN, REGION), P(REGION), P(REGION, None), P(REGION), P(REGION, None))
    out_specs = (P(REGION, None, RUN, None), P(REGION, None, None, None, None, RUN))
    return jax.shard_map(shards, mesh=fine, in_specs=in_specs, out_specs=out_specs, check_vma=False)
```

```python
import functools

import jax
import jax.numpy as jnp
from jax import lax
from jax.experimental import pallas as pl
from jax.experimental.pallas import tpu as pltpu
from jax.sharding import Mesh, PartitionSpec as P

OBS = 4
COUPLE = 2
BS = 128
SPLIT = 3
HALVES = 2
REGION = ("x", "zlo")
RUN = ("zhi", "y", "core")
MESH = pl.DeviceIdType.MESH


def remote(src, dst, send, recv, where):
    return pltpu.make_async_remote_copy(
        src_ref=src, dst_ref=dst, send_sem=send, recv_sem=recv, device_id=where, device_id_type=MESH
    )


def loop(low, high, body):
    def step(i, carry):
        body(i)
        return carry

    lax.fori_loop(low, high, step, 0)


def gather_kernel(
    sizes, sens, counts, table, acc, masked, zbuf, outbuf, inbuf, ztab, xtab, stab,
    zs, zr, ys, yr, ps, pr, tzs, tzr, txs, txr, tsem, *tbufs,
):
    nx, nz, ny, nc = sizes
    x, zlo = lax.axis_index("x"), lax.axis_index("zlo")
    y, core = lax.axis_index("y"), lax.axis_index("core")
    rho = y * nc + core
    plane = x * nz + rho
    planes = nx * nz
    depth = tbufs[0].shape[1] * tbufs[0].shape[2]
    stride = 11 % planes
    blocks, sub = masked.shape[2], masked.shape[3]
    first_run = (lax.axis_index("zhi") * nz + rho) * (sens.shape[0] // OBS)

    def z_at(d):
        return {"zlo": lax.rem(zlo + d, nz)}

    def yc_at(t):
        return {"y": t // nc, "core": lax.rem(t, nc)}

    def x_at(d):
        return {"x": lax.rem(x + d, nx)}

    def plane_at(t):
        r = lax.rem(t, nz)
        return {"x": t // nz, "y": r // nc, "core": lax.rem(r, nc)}

    barrier = pltpu.get_barrier_semaphore()
    loop(1, nz, lambda d: pl.semaphore_signal(barrier, inc=1, device_id=z_at(d), device_id_type=MESH))
    loop(1, planes, lambda g: pl.semaphore_signal(
        barrier, inc=1, device_id=plane_at(lax.rem(plane + g, planes)), device_id_type=MESH))
    pl.semaphore_wait(barrier, nz - 1 + planes - 1)

    def table_copy(d):
        return remote(table, ztab.at[zlo], tzs.at[d], tzr.at[d], z_at(d))

    def row_copy(x_from, d):
        return remote(ztab, xtab.at[x_from], txs.at[d], txr.at[d], x_at(d))

    def z_copy(s, d):
        return remote(
            masked.at[lax.rem(zlo + d, nz), s], zbuf.at[s, zlo], zs.at[s, d], zr.at[s, d], z_at(d))

    def y_copy(s, e):
        t = lax.rem(rho + e, nz)
        return remote(zbuf.at[s, t], tbufs[s].at[:, rho], ys.at[s, e], yr.at[s, e], yc_at(t))

    def p_copy(s, g):
        return remote(
            outbuf.at[s, g], inbuf.at[s, plane], ps.at[s, g], pr.at[s, g],
            plane_at(lax.rem(plane + g, planes)))

    def mask(j, s):
        start = pl.multiple_of((j * SPLIT + s) * sub, sub)
        run = (start + lax.broadcasted_iota(jnp.int32, (sub, BS), 0)) // OBS + first_run
        for b in range(blocks):
            value = sens[pl.ds(start, sub), b * BS:(b + 1) * BS].astype(jnp.float32)
            masked[j, s, b] = jnp.where(run < counts[b], value, 0.0).astype(jnp.bfloat16)

    def z_send(s):
        def one(d):
            mask(lax.rem(zlo + d, nz), s)
            z_copy(s, d).start()

        loop(1, nz, one)
        mask(zlo, s)
        pltpu.make_async_copy(masked.at[zlo, s], zbuf.at[s, zlo], zr.at[s, 0]).start()

    def z_wait(s, d):
        dst = zbuf.at[s, lax.rem(zlo + nz - d, nz)]
        pltpu.make_async_copy(dst, dst, zr.at[s, d]).wait()

    def relay(s):
        z_wait(s, lax.rem(zlo + nz - rho, nz))
        pltpu.make_async_copy(zbuf.at[s, rho], tbufs[s].at[:, rho], yr.at[s, 0]).start()

        def one(e):
            z_wait(s, lax.rem(zlo + 2 * nz - rho - e, nz))
            y_copy(s, e).start()

        loop(1, nz, one)

    def block(s, b):
        return tbufs[s][b].reshape(depth, BS)

    def asked(t):
        return stab[t // nz, lax.rem(t, nz), 0, plane]

    def pick(s):
        def ready(e):
            dst = tbufs[s].at[:, lax.rem(rho + nz - e, nz)]
            pltpu.make_async_copy(dst, dst, yr.at[s, e]).wait()

        loop(0, nz, ready)

        def one(i):
            g = lax.rem(i * stride, planes)
            outbuf[s, g] = block(s, asked(lax.rem(plane + g, planes)))
            p_copy(s, g).start()

        loop(1, planes, one)
        inbuf[s, plane] = block(s, asked(plane))

    def multiply(s):
        def product(q):
            near = jnp.concatenate(
                [block(s, stab[x, rho, 1 + c, q]) for c in range(COUPLE)], axis=1)
            value = lax.dot_general(
                inbuf[s, q], near, (((0,), (0,)), ((), ())), preferred_element_type=jnp.float32)
            if s == 0:
                acc[q] = value
            else:
                acc[q] += value

        def one(i):
            g = lax.rem(i * stride, planes)
            q = lax.rem(plane + planes - g, planes)
            dst = inbuf.at[s, q]
            pltpu.make_async_copy(dst, dst, pr.at[s, g]).wait()
            product(q)

        product(plane)
        loop(1, planes, one)

    pltpu.make_async_copy(table, ztab.at[zlo], tzr.at[0]).start()
    loop(1, nz, lambda d: table_copy(d).start())
    z_send(0)

    def table_wait(d):
        dst = ztab.at[lax.rem(zlo + nz - d, nz)]
        pltpu.make_async_copy(dst, dst, tzr.at[d]).wait()

    loop(0, nz, table_wait)
    pltpu.make_async_copy(ztab, xtab.at[x], txr.at[0]).start()
    loop(1, nx, lambda d: row_copy(x, d).start())

    for s in range(SPLIT):
        if s + 1 < SPLIT:
            z_send(s + 1)
        relay(s)
        if s == 0:
            def row_wait(d):
                dst = xtab.at[lax.rem(x + nx - d, nx)]
                pltpu.make_async_copy(dst, dst, txr.at[d]).wait()

            loop(0, nx, row_wait)
            fetch = pltpu.make_async_copy(xtab, stab, tsem)
            fetch.start()
            fetch.wait()
        pick(s)
        if s > 0:
            multiply(s - 1)
    multiply(SPLIT - 1)

    loop(1, nz, lambda d: table_copy(d).wait_send())
    loop(1, nx, lambda d: row_copy(x, d).wait_send())
    for s in range(SPLIT):
        loop(1, nz, lambda d: z_copy(s, d).wait_send())
        loop(1, nz, lambda e: y_copy(s, e).wait_send())
        loop(1, planes, lambda g: p_copy(s, g).wait_send())


def reduce_kernel(sizes, acc, fbuf, mbuf, ring, fin, rs, rr, fs, fr, ms, mr):
    nx, nz, nh, ny, nc = sizes
    x, zlo, zhi = lax.axis_index("x"), lax.axis_index("zlo"), lax.axis_index("zhi")
    y, core = lax.axis_index("y"), lax.axis_index("core")
    rho = y * nc + core
    plane = x * nz + rho
    region = x * nz + zlo
    planes = nx * nz
    runs = nh * ny * nc
    mine = zhi * nz + rho
    depth = nh * nz
    z = zhi * nz + zlo
    part = acc.shape[1] // HALVES

    def z_of(k):
        return {"zhi": k // nz, "zlo": lax.rem(k, nz)}

    def run_of(t):
        r = lax.rem(t, nz)
        return {"zhi": t // nz, "y": r // nc, "core": lax.rem(r, nc)}

    def next_to(way):
        return z_of(lax.rem(z + (1 if way == 0 else depth - 1), depth))

    def fisher_to(t):
        return {"x": x, "zlo": rho, **run_of(t)}

    def mirror_to(e, t):
        q = 2 * z + e
        return {"x": q // nz, "zlo": lax.rem(q, nz), **run_of(t)}

    def fisher_from(k):
        return {"x": x, "y": zlo // nc, "core": lax.rem(zlo, nc), **z_of(k)}

    def mirror_from(s):
        r = lax.rem(s, nz)
        return {"x": s // nz, "y": r // nc, "core": lax.rem(r, nc), **z_of(region // 2)}

    fisher_self = zlo == rho
    mirror_self = z == region // 2

    barrier = pltpu.get_barrier_semaphore()

    def greet(where):
        pl.semaphore_signal(barrier, inc=1, device_id=where, device_id_type=MESH)

    greet(next_to(0))
    greet(next_to(1))

    def greet_fisher(k):
        @pl.when(jnp.logical_not(fisher_self & (k == z)))
        def _():
            greet(fisher_from(k))

    def greet_mirror(s):
        @pl.when(jnp.logical_not(mirror_self & (s == plane)))
        def _():
            greet(mirror_from(s))

    loop(0, depth, greet_fisher)
    loop(0, planes, greet_mirror)
    pl.semaphore_wait(
        barrier,
        2 + runs + 2 * runs - fisher_self.astype(jnp.int32) - mirror_self.astype(jnp.int32))

    def rows(h):
        return pl.ds(h * part, part)

    def chunk(way, i):
        if way == 0:
            return lax.rem(z + 2 * depth - 2 - i, depth)
        return lax.rem(z + 2 + i, depth)

    def hop(way, i, h, src):
        return remote(
            src, ring.at[way, i, rows(h)], rs.at[way, i, h], rr.at[way, i, h], next_to(way))

    def first(way, h):
        return hop(way, 0, h, acc.at[2 * chunk(way, -1) + way, rows(h)])

    def later(way, i, h):
        return hop(way, i + 1, h, ring.at[way, i, rows(h)])

    def take(way, i, h):
        dst = ring.at[way, i, rows(h)]
        pltpu.make_async_copy(dst, dst, rr.at[way, i, h]).wait()
        ring[way, i, rows(h)] += acc[2 * chunk(way, i) + way, rows(h)]

    for h in range(HALVES):
        for way in range(2):
            first(way, h).start()

    def step(i):
        for h in range(HALVES):
            for way in range(2):
                take(way, i, h)
                later(way, i, h).start()

    loop(0, depth - 2, step)
    for way in range(2):
        for h in range(HALVES):
            take(way, depth - 2, h)
        total = ring[way, depth - 2].T
        slices = total.reshape(COUPLE, runs, BS // runs, BS)
        for c in range(COUPLE):
            fin[:, way, c] = slices[c]

    def out_f(t):
        return remote(fin.at[t], fbuf.at[pl.ds(2 * z, 2)], fs.at[t], fr.at[z], fisher_to(t))

    def out_m(e, t):
        return remote(fin.at[t, e], mbuf.at[plane], ms.at[e, t], mr.at[plane], mirror_to(e, t))

    def self_f():
        return pltpu.make_async_copy(fin.at[mine], fbuf.at[pl.ds(2 * z, 2)], fr.at[z])

    def self_m():
        return pltpu.make_async_copy(
            fin.at[mine, lax.rem(region, 2)], mbuf.at[plane], mr.at[plane])

    def is_self_m(e, t):
        return (2 * z + e == region) & (t == mine)

    def send(k):
        t = lax.rem(mine + k, runs)

        @pl.when(jnp.logical_not(fisher_self & (t == mine)))
        def _():
            out_f(t).start()

        for e in range(2):
            @pl.when(jnp.logical_not(is_self_m(e, t)))
            def _():
                out_m(e, t).start()

    loop(0, runs, send)

    @pl.when(fisher_self)
    def _():
        self_f().start()

    @pl.when(mirror_self)
    def _():
        self_m().start()

    def got_f(k):
        dst = fbuf.at[pl.ds(2 * k, 2)]
        pltpu.make_async_copy(dst, dst, fr.at[k]).wait()

    def got_m(s):
        dst = mbuf.at[s]
        pltpu.make_async_copy(dst, dst, mr.at[s]).wait()

    loop(0, depth, got_f)
    loop(0, planes, got_m)

    for h in range(HALVES):
        for way in range(2):
            first(way, h).wait_send()

    def sent(i):
        for h in range(HALVES):
            for way in range(2):
                later(way, i, h).wait_send()

    loop(0, depth - 2, sent)

    def sent_out(t):
        @pl.when(jnp.logical_not(fisher_self & (t == mine)))
        def _():
            out_f(t).wait_send()

        for e in range(2):
            @pl.when(jnp.logical_not(is_self_m(e, t)))
            def _():
                out_m(e, t).wait_send()

    loop(0, runs, sent_out)


def shards(sensitivity, run_counts, req_owner, req_block, coupled):
    rows_dev, cols = sensitivity.shape
    blocks = run_counts.shape[0]
    nx, nz, nh, ny, nc = (lax.axis_size(a) for a in ("x", "zlo", "zhi", "y", "core"))
    regions = nx * nz
    runs = nh * ny * nc
    sub = rows_dev // (nz * SPLIT)
    vmem = pl.BlockSpec(memory_space=pltpu.VMEM)
    dma = pltpu.SemaphoreType.DMA

    fields = jnp.concatenate([req_block[:, None], coupled], axis=1)
    hit = req_owner[:, 0][:, None] == jnp.arange(regions, dtype=jnp.int32)[None, :]
    sorted_fields = jnp.sum(jnp.where(hit[:, None, :], fields[:, :, None], 0), axis=0)
    table = jnp.pad(sorted_fields, ((0, 8 - 1 - COUPLE), (0, 128 - regions)))

    acc = pl.pallas_call(
        functools.partial(gather_kernel, (nx, nz, ny, nc)),
        out_shape=jax.ShapeDtypeStruct((regions, BS, COUPLE * BS), jnp.float32),
        in_specs=[vmem, pl.BlockSpec(memory_space=pltpu.SMEM), vmem],
        out_specs=vmem,
        scratch_shapes=[
            pltpu.VMEM((nz, SPLIT, blocks, sub, BS), jnp.bfloat16),
            pltpu.VMEM((SPLIT, nz, blocks, sub, BS), jnp.bfloat16),
            pltpu.VMEM((SPLIT, regions, nz * sub, BS), jnp.bfloat16),
            pltpu.VMEM((SPLIT, regions, nz * sub, BS), jnp.bfloat16),
            pltpu.VMEM((nz, 8, 128), jnp.int32),
            pltpu.VMEM((nx, nz, 8, 128), jnp.int32),
            pltpu.SMEM((nx, nz, 8, 128), jnp.int32),
            dma((SPLIT, nz)), dma((SPLIT, nz)),
            dma((SPLIT, nz)), dma((SPLIT, nz)),
            dma((SPLIT, regions)), dma((SPLIT, regions)),
            dma((nz,)), dma((nz,)), dma((nx,)), dma((nx,)), dma,
        ] + [pltpu.VMEM((blocks, nz, sub, BS), jnp.bfloat16)] * SPLIT,
        compiler_params=pltpu.CompilerParams(
            collective_id=0, has_side_effects=True, vmem_limit_bytes=48 << 20),
    )(sensitivity, run_counts, table)

    share = BS // runs
    depth = nh * nz
    by_owner, by_source = pl.pallas_call(
        functools.partial(reduce_kernel, (nx, nz, nh, ny, nc)),
        out_shape=[jax.ShapeDtypeStruct((regions, COUPLE, share, BS), jnp.float32)] * 2,
        in_specs=[vmem],
        out_specs=[vmem, vmem],
        scratch_shapes=[
            pltpu.VMEM((2, depth - 1, BS, COUPLE * BS), jnp.float32),
            pltpu.VMEM((runs, 2, COUPLE, share, BS), jnp.float32),
            dma((2, depth - 1, HALVES)), dma((2, depth - 1, HALVES)),
            dma((runs,)), dma((depth,)),
            dma((2, runs)), dma((regions,)),
        ],
        compiler_params=pltpu.CompilerParams(
            collective_id=1, has_side_effects=True, vmem_limit_bytes=32 << 20),
    )(acc)

    fisher = jnp.take(by_owner, req_owner[:, 0], axis=0).astype(jnp.bfloat16)
    mirror = jnp.swapaxes(by_source, 2, 3).astype(jnp.bfloat16)
    return fisher, mirror.reshape(1, regions, 1, COUPLE, BS, share)


def solution(mesh):
    fine = Mesh(mesh.devices.reshape(4, 8, 2, 4, 2), ("x", "zlo", "zhi", "y", "core"))
    return build(fine)


def build(fine):
    in_specs = (P(RUN, REGION), P(REGION), P(REGION, None), P(REGION), P(REGION, None))
    out_specs = (P(REGION, None, RUN, None), P(REGION, None, None, None, None, RUN))
    return jax.shard_map(shards, mesh=fine, in_specs=in_specs, out_specs=out_specs, check_vma=False)
```

```python
import functools

import jax
import jax.numpy as jnp
from jax import lax
from jax.experimental import pallas as pl
from jax.experimental.pallas import tpu as pltpu
from jax.sharding import Mesh, PartitionSpec as P

OBS = 4
COUPLE = 2
BS = 128
PARTS = (2, 2, 1, 1)
SPLIT = len(PARTS)
PIECES = 4
REGION = ("x", "zlo")
RUN = ("zhi", "y", "core")
MESH = pl.DeviceIdType.MESH


def remote(src, dst, send, recv, where):
    return pltpu.make_async_remote_copy(
        src_ref=src, dst_ref=dst, send_sem=send, recv_sem=recv, device_id=where, device_id_type=MESH
    )


def loop(low, high, body):
    def step(i, carry):
        body(i)
        return carry

    lax.fori_loop(low, high, step, 0)


def gather_kernel(
    sizes, sens, counts, table, acc, ztab, xtab, stab,
    zs, zr, ys, yr, ps, pr, tzs, tzr, txs, txr, tsem, *bufs,
):
    masked, zbufs, tbufs, outbufs, inbufs = (
        bufs[i * SPLIT:(i + 1) * SPLIT] for i in range(5))
    nx, nz, ny, nc = sizes
    x, zlo = lax.axis_index("x"), lax.axis_index("zlo")
    y, core = lax.axis_index("y"), lax.axis_index("core")
    rho = y * nc + core
    plane = x * nz + rho
    planes = nx * nz
    stride = 11 % planes
    blocks = masked[0].shape[1]
    sub = [m.shape[2] for m in masked]
    offset = [sum(sub[:s]) for s in range(SPLIT)]
    first_run = (lax.axis_index("zhi") * nz + rho) * (sens.shape[0] // OBS)

    def z_at(d):
        return {"zlo": lax.rem(zlo + d, nz)}

    def yc_at(t):
        return {"y": t // nc, "core": lax.rem(t, nc)}

    def x_at(d):
        return {"x": lax.rem(x + d, nx)}

    def plane_at(t):
        r = lax.rem(t, nz)
        return {"x": t // nz, "y": r // nc, "core": lax.rem(r, nc)}

    barrier = pltpu.get_barrier_semaphore()
    loop(1, nz, lambda d: pl.semaphore_signal(barrier, inc=1, device_id=z_at(d), device_id_type=MESH))
    loop(1, planes, lambda g: pl.semaphore_signal(
        barrier, inc=1, device_id=plane_at(lax.rem(plane + g, planes)), device_id_type=MESH))

    def table_copy(d):
        return remote(table, ztab.at[zlo], tzs.at[d], tzr.at[d], z_at(d))

    def row_copy(x_from, d):
        return remote(ztab, xtab.at[x_from], txs.at[d], txr.at[d], x_at(d))

    def z_copy(s, d):
        return remote(
            masked[s].at[lax.rem(zlo + d, nz)], zbufs[s].at[zlo], zs.at[s, d], zr.at[s, d], z_at(d))

    def y_copy(s, e):
        t = lax.rem(rho + e, nz)
        return remote(zbufs[s].at[t], tbufs[s].at[:, rho], ys.at[s, e], yr.at[s, e], yc_at(t))

    def p_copy(s, g):
        return remote(
            outbufs[s].at[g], inbufs[s].at[plane], ps.at[s, g], pr.at[s, g],
            plane_at(lax.rem(plane + g, planes)))

    def mask(j, s):
        start = pl.multiple_of(j * sum(sub) + offset[s], sub[-1])
        run = (start + lax.broadcasted_iota(jnp.int32, (sub[s], BS), 0)) // OBS + first_run
        for b in range(blocks):
            value = sens[pl.ds(start, sub[s]), b * BS:(b + 1) * BS].astype(jnp.float32)
            masked[s][j, b] = jnp.where(run < counts[b], value, 0.0).astype(jnp.bfloat16)

    def z_send(s):
        def one(d):
            if s > 0:
                mask(lax.rem(zlo + d, nz), s)
            z_copy(s, d).start()

        loop(1, nz, one)
        if s > 0:
            mask(zlo, s)
        pltpu.make_async_copy(masked[s].at[zlo], zbufs[s].at[zlo], zr.at[s, 0]).start()

    def z_wait(s, d):
        dst = zbufs[s].at[lax.rem(zlo + nz - d, nz)]
        pltpu.make_async_copy(dst, dst, zr.at[s, d]).wait()

    def relay(s):
        z_wait(s, lax.rem(zlo + nz - rho, nz))
        pltpu.make_async_copy(zbufs[s].at[rho], tbufs[s].at[:, rho], yr.at[s, 0]).start()

        def one(e):
            z_wait(s, lax.rem(zlo + 2 * nz - rho - e, nz))
            y_copy(s, e).start()

        loop(1, nz, one)

    def block(s, b):
        return tbufs[s][b].reshape(nz * sub[s], BS)

    def asked(t):
        return stab[t // nz, lax.rem(t, nz), 0, plane]

    def pick(s):
        def ready(e):
            dst = tbufs[s].at[:, lax.rem(rho + nz - e, nz)]
            pltpu.make_async_copy(dst, dst, yr.at[s, e]).wait()

        loop(0, nz, ready)

        def one(i):
            g = lax.rem(i * stride, planes)
            outbufs[s][g] = block(s, asked(lax.rem(plane + g, planes)))
            p_copy(s, g).start()

        loop(1, planes, one)
        inbufs[s][plane] = block(s, asked(plane))

    def multiply(s):
        def product(q):
            near = jnp.concatenate(
                [block(s, stab[x, rho, 1 + c, q]) for c in range(COUPLE)], axis=1)
            value = lax.dot_general(
                inbufs[s][q], near, (((0,), (0,)), ((), ())), preferred_element_type=jnp.float32)
            if s == 0:
                acc[q] = value
            else:
                acc[q] += value

        def one(i):
            g = lax.rem(i * stride, planes)
            q = lax.rem(plane + planes - g, planes)
            dst = inbufs[s].at[q]
            pltpu.make_async_copy(dst, dst, pr.at[s, g]).wait()
            product(q)

        product(plane)
        loop(1, planes, one)

    loop(0, nz, lambda j: mask(j, 0))
    pl.semaphore_wait(barrier, nz - 1 + planes - 1)

    pltpu.make_async_copy(table, ztab.at[zlo], tzr.at[0]).start()
    loop(1, nz, lambda d: table_copy(d).start())
    z_send(0)

    def table_wait(d):
        dst = ztab.at[lax.rem(zlo + nz - d, nz)]
        pltpu.make_async_copy(dst, dst, tzr.at[d]).wait()

    loop(0, nz, table_wait)
    pltpu.make_async_copy(ztab, xtab.at[x], txr.at[0]).start()
    loop(1, nx, lambda d: row_copy(x, d).start())

    for s in range(SPLIT):
        if s + 1 < SPLIT:
            z_send(s + 1)
        relay(s)
        if s == 0:
            def row_wait(d):
                dst = xtab.at[lax.rem(x + nx - d, nx)]
                pltpu.make_async_copy(dst, dst, txr.at[d]).wait()

            loop(0, nx, row_wait)
            fetch = pltpu.make_async_copy(xtab, stab, tsem)
            fetch.start()
            fetch.wait()
        pick(s)
        if s > 0:
            multiply(s - 1)
    multiply(SPLIT - 1)

    loop(1, nz, lambda d: table_copy(d).wait_send())
    loop(1, nx, lambda d: row_copy(x, d).wait_send())
    for s in range(SPLIT):
        loop(1, nz, lambda d: z_copy(s, d).wait_send())
        loop(1, nz, lambda e: y_copy(s, e).wait_send())
        loop(1, planes, lambda g: p_copy(s, g).wait_send())


def reduce_kernel(sizes, acc, fbuf, mbuf, ring, fin, rs, rr, fs, fr, ms, mr):
    nx, nz, nh, ny, nc = sizes
    x, zlo, zhi = lax.axis_index("x"), lax.axis_index("zlo"), lax.axis_index("zhi")
    y, core = lax.axis_index("y"), lax.axis_index("core")
    rho = y * nc + core
    plane = x * nz + rho
    region = x * nz + zlo
    planes = nx * nz
    runs = nh * ny * nc
    mine = zhi * nz + rho
    depth = nh * nz
    z = zhi * nz + zlo
    part = acc.shape[1] // PIECES

    def z_of(k):
        return {"zhi": k // nz, "zlo": lax.rem(k, nz)}

    def run_of(t):
        r = lax.rem(t, nz)
        return {"zhi": t // nz, "y": r // nc, "core": lax.rem(r, nc)}

    def next_to(way):
        return z_of(lax.rem(z + (1 if way == 0 else depth - 1), depth))

    def fisher_to(t):
        return {"x": x, "zlo": rho, **run_of(t)}

    def mirror_to(e, t):
        q = 2 * z + e
        return {"x": q // nz, "zlo": lax.rem(q, nz), **run_of(t)}

    def fisher_from(k):
        return {"x": x, "y": zlo // nc, "core": lax.rem(zlo, nc), **z_of(k)}

    def mirror_from(s):
        r = lax.rem(s, nz)
        return {"x": s // nz, "y": r // nc, "core": lax.rem(r, nc), **z_of(region // 2)}

    fisher_self = zlo == rho
    mirror_self = z == region // 2

    barrier = pltpu.get_barrier_semaphore()

    def greet(where):
        pl.semaphore_signal(barrier, inc=1, device_id=where, device_id_type=MESH)

    greet(next_to(0))
    greet(next_to(1))

    def greet_fisher(k):
        @pl.when(jnp.logical_not(fisher_self & (k == z)))
        def _():
            greet(fisher_from(k))

    def greet_mirror(s):
        @pl.when(jnp.logical_not(mirror_self & (s == plane)))
        def _():
            greet(mirror_from(s))

    loop(0, depth, greet_fisher)
    loop(0, planes, greet_mirror)
    pl.semaphore_wait(
        barrier,
        2 + runs + 2 * runs - fisher_self.astype(jnp.int32) - mirror_self.astype(jnp.int32))

    def rows(h):
        return pl.ds(h * part, part)

    def chunk(way, i):
        if way == 0:
            return lax.rem(z + 2 * depth - 2 - i, depth)
        return lax.rem(z + 2 + i, depth)

    def hop(way, i, h, src):
        return remote(
            src, ring.at[way, i, rows(h)], rs.at[way, i, h], rr.at[way, i, h], next_to(way))

    def first(way, h):
        return hop(way, 0, h, acc.at[2 * chunk(way, -1) + way, rows(h)])

    def later(way, i, h):
        return hop(way, i + 1, h, ring.at[way, i, rows(h)])

    def take(way, i, h):
        dst = ring.at[way, i, rows(h)]
        pltpu.make_async_copy(dst, dst, rr.at[way, i, h]).wait()
        ring[way, i, rows(h)] += acc[2 * chunk(way, i) + way, rows(h)]

    for h in range(PIECES):
        for way in range(2):
            first(way, h).start()

    def step(i):
        for h in range(PIECES):
            for way in range(2):
                take(way, i, h)
                later(way, i, h).start()

    loop(0, depth - 2, step)
    for way in range(2):
        for h in range(PIECES):
            take(way, depth - 2, h)
        total = ring[way, depth - 2].T
        slices = total.reshape(COUPLE, runs, BS // runs, BS)
        fin[:, way] = jnp.concatenate([slices[c] for c in range(COUPLE)], axis=1).astype(jnp.bfloat16)

    def out_f(t):
        return remote(fin.at[t], fbuf.at[pl.ds(2 * z, 2)], fs.at[t], fr.at[z], fisher_to(t))

    def out_m(e, t):
        return remote(fin.at[t, e], mbuf.at[plane], ms.at[e, t], mr.at[plane], mirror_to(e, t))

    def self_f():
        return pltpu.make_async_copy(fin.at[mine], fbuf.at[pl.ds(2 * z, 2)], fr.at[z])

    def self_m():
        return pltpu.make_async_copy(
            fin.at[mine, lax.rem(region, 2)], mbuf.at[plane], mr.at[plane])

    def is_self_m(e, t):
        return (2 * z + e == region) & (t == mine)

    def send(k):
        t = lax.rem(mine + k, runs)

        @pl.when(jnp.logical_not(fisher_self & (t == mine)))
        def _():
            out_f(t).start()

        for e in range(2):
            @pl.when(jnp.logical_not(is_self_m(e, t)))
            def _():
                out_m(e, t).start()

    loop(0, runs, send)

    @pl.when(fisher_self)
    def _():
        self_f().start()

    @pl.when(mirror_self)
    def _():
        self_m().start()

    def got_f(k):
        dst = fbuf.at[pl.ds(2 * k, 2)]
        pltpu.make_async_copy(dst, dst, fr.at[k]).wait()

    def got_m(s):
        dst = mbuf.at[s]
        pltpu.make_async_copy(dst, dst, mr.at[s]).wait()

    loop(0, depth, got_f)
    loop(0, planes, got_m)

    for h in range(PIECES):
        for way in range(2):
            first(way, h).wait_send()

    def sent(i):
        for h in range(PIECES):
            for way in range(2):
                later(way, i, h).wait_send()

    loop(0, depth - 2, sent)

    def sent_out(t):
        @pl.when(jnp.logical_not(fisher_self & (t == mine)))
        def _():
            out_f(t).wait_send()

        for e in range(2):
            @pl.when(jnp.logical_not(is_self_m(e, t)))
            def _():
                out_m(e, t).wait_send()

    loop(0, runs, sent_out)


def shards(sensitivity, run_counts, req_owner, req_block, coupled):
    rows_dev, cols = sensitivity.shape
    blocks = run_counts.shape[0]
    nx, nz, nh, ny, nc = (lax.axis_size(a) for a in ("x", "zlo", "zhi", "y", "core"))
    regions = nx * nz
    runs = nh * ny * nc
    sub = [n * rows_dev // (nz * sum(PARTS)) for n in PARTS]
    vmem = pl.BlockSpec(memory_space=pltpu.VMEM)
    dma = pltpu.SemaphoreType.DMA

    fields = jnp.concatenate([req_block[:, None], coupled], axis=1)
    hit = req_owner[:, 0][:, None] == jnp.arange(regions, dtype=jnp.int32)[None, :]
    sorted_fields = jnp.sum(jnp.where(hit[:, None, :], fields[:, :, None], 0), axis=0)
    table = jnp.pad(sorted_fields, ((0, 8 - 1 - COUPLE), (0, 128 - regions)))

    acc = pl.pallas_call(
        functools.partial(gather_kernel, (nx, nz, ny, nc)),
        out_shape=jax.ShapeDtypeStruct((regions, BS, COUPLE * BS), jnp.float32),
        in_specs=[vmem, pl.BlockSpec(memory_space=pltpu.SMEM), vmem],
        out_specs=vmem,
        scratch_shapes=[
            pltpu.VMEM((nz, 8, 128), jnp.int32),
            pltpu.VMEM((nx, nz, 8, 128), jnp.int32),
            pltpu.SMEM((nx, nz, 8, 128), jnp.int32),
            dma((SPLIT, nz)), dma((SPLIT, nz)),
            dma((SPLIT, nz)), dma((SPLIT, nz)),
            dma((SPLIT, regions)), dma((SPLIT, regions)),
            dma((nz,)), dma((nz,)), dma((nx,)), dma((nx,)), dma,
        ] + [
            pltpu.VMEM(shape, jnp.bfloat16)
            for shape in (
                [(nz, blocks, n, BS) for n in sub] * 2
                + [(blocks, nz, n, BS) for n in sub]
                + [(regions, nz * n, BS) for n in sub] * 2)
        ],
        compiler_params=pltpu.CompilerParams(
            collective_id=0, has_side_effects=True, vmem_limit_bytes=48 << 20),
    )(sensitivity, run_counts, table)

    share = BS // runs
    depth = nh * nz
    by_owner, by_source = pl.pallas_call(
        functools.partial(reduce_kernel, (nx, nz, nh, ny, nc)),
        out_shape=[jax.ShapeDtypeStruct((regions, COUPLE * share, BS), jnp.bfloat16)] * 2,
        in_specs=[vmem],
        out_specs=[vmem, vmem],
        scratch_shapes=[
            pltpu.VMEM((2, depth - 1, BS, COUPLE * BS), jnp.float32),
            pltpu.VMEM((runs, 2, COUPLE * share, BS), jnp.bfloat16),
            dma((2, depth - 1, PIECES)), dma((2, depth - 1, PIECES)),
            dma((runs,)), dma((depth,)),
            dma((2, runs)), dma((regions,)),
        ],
        compiler_params=pltpu.CompilerParams(
            collective_id=1, has_side_effects=True, vmem_limit_bytes=32 << 20),
    )(acc)

    fisher = jnp.take(by_owner, req_owner[:, 0], axis=0).reshape(-1, COUPLE, share, BS)
    mirror = jnp.swapaxes(by_source.reshape(-1, COUPLE, share, BS), 2, 3)
    return fisher, mirror.reshape(1, regions, 1, COUPLE, BS, share)


def solution(mesh):
    fine = Mesh(mesh.devices.reshape(4, 8, 2, 4, 2), ("x", "zlo", "zhi", "y", "core"))
    return build(fine)


def build(fine):
    in_specs = (P(RUN, REGION), P(REGION), P(REGION, None), P(REGION), P(REGION, None))
    out_specs = (P(REGION, None, RUN, None), P(REGION, None, None, None, None, RUN))
    return jax.shard_map(shards, mesh=fine, in_specs=in_specs, out_specs=out_specs, check_vma=False)
```

```python
import functools

import jax
import jax.numpy as jnp
from jax import lax
from jax.experimental import pallas as pl
from jax.experimental.pallas import tpu as pltpu
from jax.sharding import Mesh, PartitionSpec as P

OBS = 4
COUPLE = 2
BS = 128
PARTS = (2, 2, 1, 1)
SPLIT = len(PARTS)
PIECES = 4
REGION = ("x", "zlo")
RUN = ("zhi", "y", "core")
MESH = pl.DeviceIdType.MESH


def remote(src, dst, send, recv, where):
    return pltpu.make_async_remote_copy(
        src_ref=src, dst_ref=dst, send_sem=send, recv_sem=recv, device_id=where, device_id_type=MESH
    )


def loop(low, high, body):
    def step(i, carry):
        body(i)
        return carry

    lax.fori_loop(low, high, step, 0)


def gather_kernel(
    sizes, sens, counts, table, acc, ztab, xtab, stab,
    zs, zr, ys, yr, ps, pr, tzs, tzr, txs, txr, tsem, *bufs,
):
    masked, zbufs, tbufs, turned, outbufs, inbufs = (
        bufs[i * SPLIT:(i + 1) * SPLIT] for i in range(6))
    nx, nz, ny, nc = sizes
    x, zlo = lax.axis_index("x"), lax.axis_index("zlo")
    y, core = lax.axis_index("y"), lax.axis_index("core")
    rho = y * nc + core
    plane = x * nz + rho
    planes = nx * nz
    stride = 11 % planes
    blocks = masked[0].shape[1]
    sub = [m.shape[2] for m in masked]
    offset = [sum(sub[:s]) for s in range(SPLIT)]
    first_run = (lax.axis_index("zhi") * nz + rho) * (sens.shape[0] // OBS)

    def z_at(d):
        return {"zlo": lax.rem(zlo + d, nz)}

    def yc_at(t):
        return {"y": t // nc, "core": lax.rem(t, nc)}

    def x_at(d):
        return {"x": lax.rem(x + d, nx)}

    def plane_at(t):
        r = lax.rem(t, nz)
        return {"x": t // nz, "y": r // nc, "core": lax.rem(r, nc)}

    barrier = pltpu.get_barrier_semaphore()
    loop(1, nz, lambda d: pl.semaphore_signal(barrier, inc=1, device_id=z_at(d), device_id_type=MESH))
    loop(1, planes, lambda g: pl.semaphore_signal(
        barrier, inc=1, device_id=plane_at(lax.rem(plane + g, planes)), device_id_type=MESH))

    def table_copy(d):
        return remote(table, ztab.at[zlo], tzs.at[d], tzr.at[d], z_at(d))

    def row_copy(x_from, d):
        return remote(ztab, xtab.at[x_from], txs.at[d], txr.at[d], x_at(d))

    def z_copy(s, d):
        return remote(
            masked[s].at[lax.rem(zlo + d, nz)], zbufs[s].at[zlo], zs.at[s, d], zr.at[s, d], z_at(d))

    def y_copy(s, e):
        t = lax.rem(rho + e, nz)
        return remote(zbufs[s].at[t], tbufs[s].at[:, rho], ys.at[s, e], yr.at[s, e], yc_at(t))

    def p_copy(s, g):
        return remote(
            outbufs[s].at[g], inbufs[s].at[plane], ps.at[s, g], pr.at[s, g],
            plane_at(lax.rem(plane + g, planes)))

    def mask(j, s):
        start = pl.multiple_of(j * sum(sub) + offset[s], sub[-1])
        run = (start + lax.broadcasted_iota(jnp.int32, (sub[s], BS), 0)) // OBS + first_run
        for b in range(blocks):
            value = sens[pl.ds(start, sub[s]), b * BS:(b + 1) * BS].astype(jnp.float32)
            masked[s][j, b] = jnp.where(run < counts[b], value, 0.0).astype(jnp.bfloat16)

    def z_send(s):
        def one(i):
            d = lax.rem(i * 3, nz)
            if s > 0:
                mask(lax.rem(zlo + d, nz), s)
            z_copy(s, d).start()

        loop(1, nz, one)
        if s > 0:
            mask(zlo, s)
        pltpu.make_async_copy(masked[s].at[zlo], zbufs[s].at[zlo], zr.at[s, 0]).start()

    def z_wait(s, d):
        dst = zbufs[s].at[lax.rem(zlo + nz - d, nz)]
        pltpu.make_async_copy(dst, dst, zr.at[s, d]).wait()

    def relay(s):
        def one(i):
            d = lax.rem(i * 3, nz)
            z_wait(s, d)
            e = lax.rem(zlo + 2 * nz - d - rho, nz)

            @pl.when(e == 0)
            def _():
                pltpu.make_async_copy(zbufs[s].at[rho], tbufs[s].at[:, rho], yr.at[s, 0]).start()

            @pl.when(e > 0)
            def _():
                y_copy(s, e).start()

        loop(0, nz, one)

    def block(s, b):
        return tbufs[s][b].reshape(nz * sub[s], BS)

    def asked(t):
        return stab[t // nz, lax.rem(t, nz), 0, plane]

    def pick(s):
        def ready(e):
            dst = tbufs[s].at[:, lax.rem(rho + nz - e, nz)]
            pltpu.make_async_copy(dst, dst, yr.at[s, e]).wait()

        loop(0, nz, ready)

        def one(i):
            g = lax.rem(i * stride, planes)
            outbufs[s][g] = block(s, asked(lax.rem(plane + g, planes)))
            p_copy(s, g).start()

        loop(1, planes, one)
        inbufs[s][plane] = block(s, asked(plane))

    def turn(s):
        def one(b):
            turned[s][b] = tbufs[s][b].reshape(nz * sub[s], BS).T

        loop(0, blocks, one)

    def multiply(s):
        def product(q):
            near = jnp.concatenate(
                [turned[s][stab[x, rho, 1 + c, q]] for c in range(COUPLE)], axis=0)
            value = jnp.dot(near, inbufs[s][q], preferred_element_type=jnp.float32)
            if s == 0:
                acc[q] = value
            else:
                acc[q] += value

        def one(i):
            g = lax.rem(i * stride, planes)
            q = lax.rem(plane + planes - g, planes)
            dst = inbufs[s].at[q]
            pltpu.make_async_copy(dst, dst, pr.at[s, g]).wait()
            product(q)

        product(plane)
        loop(1, planes, one)

    loop(0, nz, lambda j: mask(j, 0))
    pl.semaphore_wait(barrier, nz - 1 + planes - 1)

    pltpu.make_async_copy(table, ztab.at[zlo], tzr.at[0]).start()
    loop(1, nz, lambda d: table_copy(d).start())
    z_send(0)

    def table_wait(d):
        dst = ztab.at[lax.rem(zlo + nz - d, nz)]
        pltpu.make_async_copy(dst, dst, tzr.at[d]).wait()

    z_send(1)
    loop(0, nz, table_wait)
    pltpu.make_async_copy(ztab, xtab.at[x], txr.at[0]).start()
    loop(1, nx, lambda d: row_copy(x, d).start())

    for s in range(SPLIT):
        if s + 2 < SPLIT:
            z_send(s + 2)
        relay(s)
        if s > 0:
            multiply(s - 1)
        if s == 0:
            def row_wait(d):
                dst = xtab.at[lax.rem(x + nx - d, nx)]
                pltpu.make_async_copy(dst, dst, txr.at[d]).wait()

            loop(0, nx, row_wait)
            fetch = pltpu.make_async_copy(xtab, stab, tsem)
            fetch.start()
            fetch.wait()
        pick(s)
        turn(s)
    multiply(SPLIT - 1)

    loop(1, nz, lambda d: table_copy(d).wait_send())
    loop(1, nx, lambda d: row_copy(x, d).wait_send())
    for s in range(SPLIT):
        loop(1, nz, lambda d: z_copy(s, d).wait_send())
        loop(1, nz, lambda e: y_copy(s, e).wait_send())
        loop(1, planes, lambda g: p_copy(s, g).wait_send())


def reduce_kernel(sizes, acc, fbuf, mbuf, ring, fin, rs, rr, fs, fr, ms, mr):
    nx, nz, nh, ny, nc = sizes
    x, zlo, zhi = lax.axis_index("x"), lax.axis_index("zlo"), lax.axis_index("zhi")
    y, core = lax.axis_index("y"), lax.axis_index("core")
    rho = y * nc + core
    plane = x * nz + rho
    region = x * nz + zlo
    planes = nx * nz
    runs = nh * ny * nc
    mine = zhi * nz + rho
    depth = nh * nz
    z = zhi * nz + zlo
    ahead = [depth // 2, depth - 1 - depth // 2]
    pieces = [(e, h) for h in range(PIECES // 2) for e in range(2)]
    part = acc.shape[1] // (PIECES // 2)

    def z_of(k):
        return {"zhi": k // nz, "zlo": lax.rem(k, nz)}

    def run_of(t):
        r = lax.rem(t, nz)
        return {"zhi": t // nz, "y": r // nc, "core": lax.rem(r, nc)}

    def next_to(way):
        return z_of(lax.rem(z + (1 if way == 0 else depth - 1), depth))

    def fisher_to(t):
        return {"x": x, "zlo": rho, **run_of(t)}

    def mirror_to(e, t):
        q = 2 * z + e
        return {"x": q // nz, "zlo": lax.rem(q, nz), **run_of(t)}

    def fisher_from(k):
        return {"x": x, "y": zlo // nc, "core": lax.rem(zlo, nc), **z_of(k)}

    def mirror_from(s):
        r = lax.rem(s, nz)
        return {"x": s // nz, "y": r // nc, "core": lax.rem(r, nc), **z_of(region // 2)}

    fisher_self = zlo == rho
    mirror_self = z == region // 2

    barrier = pltpu.get_barrier_semaphore()

    def greet(where):
        pl.semaphore_signal(barrier, inc=1, device_id=where, device_id_type=MESH)

    greet(next_to(0))
    greet(next_to(1))

    def greet_fisher(k):
        @pl.when(jnp.logical_not(fisher_self & (k == z)))
        def _():
            greet(fisher_from(k))

    def greet_mirror(s):
        @pl.when(jnp.logical_not(mirror_self & (s == plane)))
        def _():
            greet(mirror_from(s))

    loop(0, depth, greet_fisher)
    loop(0, planes, greet_mirror)
    pl.semaphore_wait(
        barrier,
        2 + runs + 2 * runs - fisher_self.astype(jnp.int32) - mirror_self.astype(jnp.int32))

    def rows(h):
        return pl.ds(h * part, part)

    def chunk(way, i):
        if way == 0:
            return lax.rem(z + depth - 1 + ahead[0] - i, depth)
        return lax.rem(z + depth + 1 - ahead[1] + i, depth)

    def hop(way, i, p, src):
        e, h = pieces[p]
        return remote(
            src, ring.at[way, i, e, rows(h)], rs.at[way, i, p], rr.at[way, i, p], next_to(way))

    def first(way, p):
        e, h = pieces[p]
        own = lax.rem(z + depth + (ahead[0] if way == 0 else -ahead[1]), depth)
        return hop(way, 0, p, acc.at[2 * own + e, rows(h)])

    def later(way, i, p):
        e, h = pieces[p]
        return hop(way, i + 1, p, ring.at[way, i, e, rows(h)])

    def arrive(way, i, p):
        e, h = pieces[p]
        dst = ring.at[way, i, e, rows(h)]
        pltpu.make_async_copy(dst, dst, rr.at[way, i, p]).wait()

    def step(i, ways):
        for p, (e, h) in enumerate(pieces):
            for way in ways:
                arrive(way, i, p)
                ring[way, i, e, rows(h)] += acc[2 * chunk(way, i) + e, rows(h)]
                later(way, i, p).start()

    ways = [way for way in range(2) if ahead[way] > 0]
    both = max(0, ahead[1] - 1)
    for p in range(len(pieces)):
        for way in ways:
            first(way, p).start()
    loop(0, both, lambda i: step(i, [0, 1]))
    for i in range(both, ahead[0] - 1):
        step(i, [0])
    for way in ways:
        for p in range(len(pieces)):
            arrive(way, ahead[way] - 1, p)
    for e in range(2):
        total = acc[2 * z + e]
        for way in ways:
            total += ring[way, ahead[way] - 1, e]
        slices = total.reshape(COUPLE, runs, BS // runs, BS)
        fin[:, e] = jnp.concatenate([slices[c] for c in range(COUPLE)], axis=1).astype(jnp.bfloat16)

    def out_f(t):
        return remote(fin.at[t], fbuf.at[pl.ds(2 * z, 2)], fs.at[t], fr.at[z], fisher_to(t))

    def out_m(e, t):
        return remote(fin.at[t, e], mbuf.at[plane], ms.at[e, t], mr.at[plane], mirror_to(e, t))

    def self_f():
        return pltpu.make_async_copy(fin.at[mine], fbuf.at[pl.ds(2 * z, 2)], fr.at[z])

    def self_m():
        return pltpu.make_async_copy(
            fin.at[mine, lax.rem(region, 2)], mbuf.at[plane], mr.at[plane])

    def is_self_m(e, t):
        return (2 * z + e == region) & (t == mine)

    def send(k):
        t = lax.rem(mine + k, runs)

        @pl.when(jnp.logical_not(fisher_self & (t == mine)))
        def _():
            out_f(t).start()

        for e in range(2):
            @pl.when(jnp.logical_not(is_self_m(e, t)))
            def _():
                out_m(e, t).start()

    loop(0, runs, send)

    @pl.when(fisher_self)
    def _():
        self_f().start()

    @pl.when(mirror_self)
    def _():
        self_m().start()

    def got_f(k):
        dst = fbuf.at[pl.ds(2 * k, 2)]
        pltpu.make_async_copy(dst, dst, fr.at[k]).wait()

    def got_m(s):
        dst = mbuf.at[s]
        pltpu.make_async_copy(dst, dst, mr.at[s]).wait()

    loop(0, depth, got_f)
    loop(0, planes, got_m)

    for p in range(len(pieces)):
        for way in ways:
            first(way, p).wait_send()

    def sent(way, i):
        for p in range(len(pieces)):
            later(way, i, p).wait_send()

    for way in ways:
        loop(0, ahead[way] - 1, functools.partial(sent, way))

    def sent_out(t):
        @pl.when(jnp.logical_not(fisher_self & (t == mine)))
        def _():
            out_f(t).wait_send()

        for e in range(2):
            @pl.when(jnp.logical_not(is_self_m(e, t)))
            def _():
                out_m(e, t).wait_send()

    loop(0, runs, sent_out)


def shards(sensitivity, run_counts, req_owner, req_block, coupled):
    rows_dev, cols = sensitivity.shape
    blocks = run_counts.shape[0]
    nx, nz, nh, ny, nc = (lax.axis_size(a) for a in ("x", "zlo", "zhi", "y", "core"))
    regions = nx * nz
    runs = nh * ny * nc
    sub = [n * rows_dev // (nz * sum(PARTS)) for n in PARTS]
    vmem = pl.BlockSpec(memory_space=pltpu.VMEM)
    dma = pltpu.SemaphoreType.DMA

    fields = jnp.concatenate([req_block[:, None], coupled], axis=1)
    hit = req_owner[:, 0][:, None] == jnp.arange(regions, dtype=jnp.int32)[None, :]
    sorted_fields = jnp.sum(jnp.where(hit[:, None, :], fields[:, :, None], 0), axis=0)
    table = jnp.pad(sorted_fields, ((0, 8 - 1 - COUPLE), (0, 128 - regions)))

    acc = pl.pallas_call(
        functools.partial(gather_kernel, (nx, nz, ny, nc)),
        out_shape=jax.ShapeDtypeStruct((regions, COUPLE * BS, BS), jnp.float32),
        in_specs=[vmem, pl.BlockSpec(memory_space=pltpu.SMEM), vmem],
        out_specs=vmem,
        scratch_shapes=[
            pltpu.VMEM((nz, 8, 128), jnp.int32),
            pltpu.VMEM((nx, nz, 8, 128), jnp.int32),
            pltpu.SMEM((nx, nz, 8, 128), jnp.int32),
            dma((SPLIT, nz)), dma((SPLIT, nz)),
            dma((SPLIT, nz)), dma((SPLIT, nz)),
            dma((SPLIT, regions)), dma((SPLIT, regions)),
            dma((nz,)), dma((nz,)), dma((nx,)), dma((nx,)), dma,
        ] + [
            pltpu.VMEM(shape, jnp.bfloat16)
            for shape in (
                [(nz, blocks, n, BS) for n in sub] * 2
                + [(blocks, nz, n, BS) for n in sub]
                + [(blocks, BS, nz * n) for n in sub]
                + [(regions, nz * n, BS) for n in sub] * 2)
        ],
        compiler_params=pltpu.CompilerParams(
            collective_id=0, has_side_effects=True, vmem_limit_bytes=48 << 20),
    )(sensitivity, run_counts, table)

    share = BS // runs
    depth = nh * nz
    by_owner, by_source = pl.pallas_call(
        functools.partial(reduce_kernel, (nx, nz, nh, ny, nc)),
        out_shape=[jax.ShapeDtypeStruct((regions, COUPLE * share, BS), jnp.bfloat16)] * 2,
        in_specs=[vmem],
        out_specs=[vmem, vmem],
        scratch_shapes=[
            pltpu.VMEM((2, depth // 2, 2, COUPLE * BS, BS), jnp.float32),
            pltpu.VMEM((runs, 2, COUPLE * share, BS), jnp.bfloat16),
            dma((2, depth // 2, PIECES)), dma((2, depth // 2, PIECES)),
            dma((runs,)), dma((depth,)),
            dma((2, runs)), dma((regions,)),
        ],
        compiler_params=pltpu.CompilerParams(
            collective_id=1, has_side_effects=True, vmem_limit_bytes=32 << 20),
    )(acc)

    fisher = jnp.take(by_owner, req_owner[:, 0], axis=0).reshape(-1, COUPLE, share, BS)
    mirror = jnp.swapaxes(by_source.reshape(-1, COUPLE, share, BS), 2, 3)
    return fisher, mirror.reshape(1, regions, 1, COUPLE, BS, share)


def solution(mesh):
    fine = Mesh(mesh.devices.reshape(4, 8, 2, 4, 2), ("x", "zlo", "zhi", "y", "core"))
    return build(fine)


def build(fine):
    in_specs = (P(RUN, REGION), P(REGION), P(REGION, None), P(REGION), P(REGION, None))
    out_specs = (P(REGION, None, RUN, None), P(REGION, None, None, None, None, RUN))
    return jax.shard_map(shards, mesh=fine, in_specs=in_specs, out_specs=out_specs, check_vma=False)
```

```python
import functools

import jax
import jax.numpy as jnp
from jax import lax
from jax.experimental import pallas as pl
from jax.experimental.pallas import tpu as pltpu
from jax.sharding import Mesh, PartitionSpec as P

OBS = 4
COUPLE = 2
BS = 128
PARTS = (1, 2, 2, 1)
SPLIT = len(PARTS)
PIECES = 8
REGION = ("x", "zlo")
RUN = ("zhi", "y", "core")
MESH = pl.DeviceIdType.MESH


def remote(src, dst, send, recv, where):
    return pltpu.make_async_remote_copy(
        src_ref=src, dst_ref=dst, send_sem=send, recv_sem=recv, device_id=where, device_id_type=MESH
    )


def loop(low, high, body):
    def step(i, carry):
        body(i)
        return carry

    lax.fori_loop(low, high, step, 0)


def gather_kernel(
    sizes, sens, counts, table, acc, ztab, xtab, stab,
    zs, zr, ys, yr, ps, pr, tzs, tzr, txs, txr, tsem, *bufs,
):
    masked, zbufs, tbufs, turned, outbufs, inbufs = (
        bufs[i * SPLIT:(i + 1) * SPLIT] for i in range(6))
    nx, nz, ny, nc = sizes
    x, zlo = lax.axis_index("x"), lax.axis_index("zlo")
    y, core = lax.axis_index("y"), lax.axis_index("core")
    rho = y * nc + core
    plane = x * nz + rho
    planes = nx * nz
    stride = 11 % planes
    blocks = masked[0].shape[1]
    sub = [m.shape[2] for m in masked]
    offset = [sum(sub[:s]) for s in range(SPLIT)]
    first_run = (lax.axis_index("zhi") * nz + rho) * (sens.shape[0] // OBS)

    def z_at(d):
        return {"zlo": lax.rem(zlo + d, nz)}

    def yc_at(t):
        return {"y": t // nc, "core": lax.rem(t, nc)}

    def x_at(d):
        return {"x": lax.rem(x + d, nx)}

    def plane_at(t):
        r = lax.rem(t, nz)
        return {"x": t // nz, "y": r // nc, "core": lax.rem(r, nc)}

    barrier = pltpu.get_barrier_semaphore()
    loop(1, nz, lambda d: pl.semaphore_signal(barrier, inc=1, device_id=z_at(d), device_id_type=MESH))
    loop(1, planes, lambda g: pl.semaphore_signal(
        barrier, inc=1, device_id=plane_at(lax.rem(plane + g, planes)), device_id_type=MESH))

    def table_copy(d):
        return remote(table, ztab.at[zlo], tzs.at[d], tzr.at[d], z_at(d))

    def row_copy(x_from, d):
        return remote(ztab, xtab.at[x_from], txs.at[d], txr.at[d], x_at(d))

    def z_copy(s, d):
        return remote(
            masked[s].at[lax.rem(zlo + d, nz)], zbufs[s].at[zlo], zs.at[s, d], zr.at[s, d], z_at(d))

    def y_copy(s, e):
        t = lax.rem(rho + e, nz)
        return remote(zbufs[s].at[t], tbufs[s].at[:, rho], ys.at[s, e], yr.at[s, e], yc_at(t))

    def p_copy(s, g):
        return remote(
            outbufs[s].at[g], inbufs[s].at[plane], ps.at[s, g], pr.at[s, g],
            plane_at(lax.rem(plane + g, planes)))

    def mask(j, s):
        start = pl.multiple_of(j * sum(sub) + offset[s], sub[-1])
        run = (start + lax.broadcasted_iota(jnp.int32, (sub[s], BS), 0)) // OBS + first_run
        for b in range(blocks):
            value = sens[pl.ds(start, sub[s]), b * BS:(b + 1) * BS].astype(jnp.float32)
            masked[s][j, b] = jnp.where(run < counts[b], value, 0.0).astype(jnp.bfloat16)

    early = min(nz // 2, nz - 1)

    def z_self(s):
        mask(zlo, s)
        pltpu.make_async_copy(masked[s].at[zlo], zbufs[s].at[zlo], zr.at[s, 0]).start()

    def z_one(s, i):
        d = lax.rem(i * 3, nz)
        mask(lax.rem(zlo + d, nz), s)
        z_copy(s, d).start()

    def z_wait(s, d):
        dst = zbufs[s].at[lax.rem(zlo + nz - d, nz)]
        pltpu.make_async_copy(dst, dst, zr.at[s, d]).wait()

    def relay(s):
        def one(i):
            d = lax.rem(i * 3, nz)
            z_wait(s, d)
            e = lax.rem(zlo + 2 * nz - d - rho, nz)

            @pl.when(e == 0)
            def _():
                pltpu.make_async_copy(zbufs[s].at[rho], tbufs[s].at[:, rho], yr.at[s, 0]).start()

            @pl.when(e > 0)
            def _():
                y_copy(s, e).start()

        if s + 1 < SPLIT:
            def both(i):
                one(i)
                z_one(s + 1, i + 1)

            loop(0, early, both)
            loop(early, nz, one)
            z_self(s + 1)
        else:
            loop(0, nz, one)

    def block(s, b):
        return tbufs[s][b].reshape(nz * sub[s], BS)

    def asked(t):
        return stab[t // nz, lax.rem(t, nz), 0, plane]

    def pick(s):
        def ready(e):
            dst = tbufs[s].at[:, lax.rem(rho + nz - e, nz)]
            pltpu.make_async_copy(dst, dst, yr.at[s, e]).wait()

        loop(0, nz, ready)

        def one(i):
            g = lax.rem(i * stride, planes)
            outbufs[s][g] = block(s, asked(lax.rem(plane + g, planes)))
            p_copy(s, g).start()

        groups = nz - 1 - early if s + 1 < SPLIT else 0
        begin = 1
        for j in range(groups):
            end = 1 + (planes - 1) * (j + 1) // (groups + 1)
            loop(begin, end, one)
            z_one(s + 1, early + 1 + j)
            begin = end
        loop(begin, planes, one)
        inbufs[s][plane] = block(s, asked(plane))

    def turn(s):
        def one(b):
            turned[s][b] = tbufs[s][b].reshape(nz * sub[s], BS).T

        loop(0, blocks, one)

    def multiply(s):
        def product(q):
            near = jnp.concatenate(
                [turned[s][stab[x, rho, 1 + c, q]] for c in range(COUPLE)], axis=0)
            value = jnp.dot(near, inbufs[s][q], preferred_element_type=jnp.float32)
            if s == 0:
                acc[q] = value
            else:
                acc[q] += value

        def one(i):
            g = lax.rem(i * stride, planes)
            q = lax.rem(plane + planes - g, planes)
            dst = inbufs[s].at[q]
            pltpu.make_async_copy(dst, dst, pr.at[s, g]).wait()
            product(q)

        product(plane)
        loop(1, planes, one)

    pl.semaphore_wait(barrier, nz - 1 + planes - 1)

    pltpu.make_async_copy(table, ztab.at[zlo], tzr.at[0]).start()
    loop(1, nz, lambda d: table_copy(d).start())
    loop(1, nz, lambda i: z_one(0, i))
    z_self(0)

    def table_wait(d):
        dst = ztab.at[lax.rem(zlo + nz - d, nz)]
        pltpu.make_async_copy(dst, dst, tzr.at[d]).wait()

    loop(0, nz, table_wait)
    pltpu.make_async_copy(ztab, xtab.at[x], txr.at[0]).start()
    loop(1, nx, lambda d: row_copy(x, d).start())

    for s in range(SPLIT):
        relay(s)
        if s > 0:
            multiply(s - 1)
        if s == 0:
            def row_wait(d):
                dst = xtab.at[lax.rem(x + nx - d, nx)]
                pltpu.make_async_copy(dst, dst, txr.at[d]).wait()

            loop(0, nx, row_wait)
            fetch = pltpu.make_async_copy(xtab, stab, tsem)
            fetch.start()
            fetch.wait()
        pick(s)
        turn(s)
    multiply(SPLIT - 1)

    loop(1, nz, lambda d: table_copy(d).wait_send())
    loop(1, nx, lambda d: row_copy(x, d).wait_send())
    for s in range(SPLIT):
        loop(1, nz, lambda d: z_copy(s, d).wait_send())
        loop(1, nz, lambda e: y_copy(s, e).wait_send())
        loop(1, planes, lambda g: p_copy(s, g).wait_send())


def reduce_kernel(sizes, acc, fbuf, mbuf, ring, fin, rs, rr, fs, fr, ms, mr):
    nx, nz, nh, ny, nc = sizes
    x, zlo, zhi = lax.axis_index("x"), lax.axis_index("zlo"), lax.axis_index("zhi")
    y, core = lax.axis_index("y"), lax.axis_index("core")
    rho = y * nc + core
    plane = x * nz + rho
    region = x * nz + zlo
    planes = nx * nz
    runs = nh * ny * nc
    mine = zhi * nz + rho
    depth = nh * nz
    z = zhi * nz + zlo
    ahead = [depth // 2, depth - 1 - depth // 2]
    pieces = [(e, h) for h in range(PIECES // 2) for e in range(2)]
    part = acc.shape[1] // (PIECES // 2)

    def z_of(k):
        return {"zhi": k // nz, "zlo": lax.rem(k, nz)}

    def run_of(t):
        r = lax.rem(t, nz)
        return {"zhi": t // nz, "y": r // nc, "core": lax.rem(r, nc)}

    def next_to(way):
        return z_of(lax.rem(z + (1 if way == 0 else depth - 1), depth))

    def fisher_to(t):
        return {"x": x, "zlo": rho, **run_of(t)}

    def mirror_to(e, t):
        q = 2 * z + e
        return {"x": q // nz, "zlo": lax.rem(q, nz), **run_of(t)}

    def fisher_from(k):
        return {"x": x, "y": zlo // nc, "core": lax.rem(zlo, nc), **z_of(k)}

    def mirror_from(s):
        r = lax.rem(s, nz)
        return {"x": s // nz, "y": r // nc, "core": lax.rem(r, nc), **z_of(region // 2)}

    fisher_self = zlo == rho
    mirror_self = z == region // 2

    barrier = pltpu.get_barrier_semaphore()

    def greet(where):
        pl.semaphore_signal(barrier, inc=1, device_id=where, device_id_type=MESH)

    greet(next_to(0))
    greet(next_to(1))

    def greet_fisher(k):
        @pl.when(jnp.logical_not(fisher_self & (k == z)))
        def _():
            greet(fisher_from(k))

    def greet_mirror(s):
        @pl.when(jnp.logical_not(mirror_self & (s == plane)))
        def _():
            greet(mirror_from(s))

    loop(0, depth, greet_fisher)
    loop(0, planes, greet_mirror)
    pl.semaphore_wait(
        barrier,
        2 + runs + 2 * runs - fisher_self.astype(jnp.int32) - mirror_self.astype(jnp.int32))

    def rows(h):
        return pl.ds(h * part, part)

    def chunk(way, i):
        if way == 0:
            return lax.rem(z + depth - 1 + ahead[0] - i, depth)
        return lax.rem(z + depth + 1 - ahead[1] + i, depth)

    def hop(way, i, p, src):
        e, h = pieces[p]
        return remote(
            src, ring.at[way, i, e, rows(h)], rs.at[way, i, p], rr.at[way, i, p], next_to(way))

    def first(way, p):
        e, h = pieces[p]
        own = lax.rem(z + depth + (ahead[0] if way == 0 else -ahead[1]), depth)
        return hop(way, 0, p, acc.at[2 * own + e, rows(h)])

    def later(way, i, p):
        e, h = pieces[p]
        return hop(way, i + 1, p, ring.at[way, i, e, rows(h)])

    def arrive(way, i, p):
        e, h = pieces[p]
        dst = ring.at[way, i, e, rows(h)]
        pltpu.make_async_copy(dst, dst, rr.at[way, i, p]).wait()

    def step(i, ways):
        for p, (e, h) in enumerate(pieces):
            for way in ways:
                arrive(way, i, p)
                ring[way, i, e, rows(h)] += acc[2 * chunk(way, i) + e, rows(h)]
                later(way, i, p).start()

    ways = [way for way in range(2) if ahead[way] > 0]
    both = max(0, ahead[1] - 1)
    for p in range(len(pieces)):
        for way in ways:
            first(way, p).start()
    loop(0, both, lambda i: step(i, [0, 1]))
    for i in range(both, ahead[0] - 1):
        step(i, [0])
    for way in ways:
        for p in range(len(pieces)):
            arrive(way, ahead[way] - 1, p)
    for e in range(2):
        total = acc[2 * z + e]
        for way in ways:
            total += ring[way, ahead[way] - 1, e]
        slices = total.reshape(COUPLE, runs, BS // runs, BS)
        fin[:, e] = jnp.concatenate([slices[c] for c in range(COUPLE)], axis=1).astype(jnp.bfloat16)

    def out_f(t):
        return remote(fin.at[t], fbuf.at[pl.ds(2 * z, 2)], fs.at[t], fr.at[z], fisher_to(t))

    def out_m(e, t):
        return remote(fin.at[t, e], mbuf.at[plane], ms.at[e, t], mr.at[plane], mirror_to(e, t))

    def self_f():
        return pltpu.make_async_copy(fin.at[mine], fbuf.at[pl.ds(2 * z, 2)], fr.at[z])

    def self_m():
        return pltpu.make_async_copy(
            fin.at[mine, lax.rem(region, 2)], mbuf.at[plane], mr.at[plane])

    def is_self_m(e, t):
        return (2 * z + e == region) & (t == mine)

    def send(k):
        t = lax.rem(mine + k, runs)

        @pl.when(jnp.logical_not(fisher_self & (t == mine)))
        def _():
            out_f(t).start()

        for e in range(2):
            @pl.when(jnp.logical_not(is_self_m(e, t)))
            def _():
                out_m(e, t).start()

    loop(0, runs, send)

    @pl.when(fisher_self)
    def _():
        self_f().start()

    @pl.when(mirror_self)
    def _():
        self_m().start()

    def got_f(k):
        dst = fbuf.at[pl.ds(2 * k, 2)]
        pltpu.make_async_copy(dst, dst, fr.at[k]).wait()

    def got_m(s):
        dst = mbuf.at[s]
        pltpu.make_async_copy(dst, dst, mr.at[s]).wait()

    loop(0, depth, got_f)
    loop(0, planes, got_m)

    for p in range(len(pieces)):
        for way in ways:
            first(way, p).wait_send()

    def sent(way, i):
        for p in range(len(pieces)):
            later(way, i, p).wait_send()

    for way in ways:
        loop(0, ahead[way] - 1, functools.partial(sent, way))

    def sent_out(t):
        @pl.when(jnp.logical_not(fisher_self & (t == mine)))
        def _():
            out_f(t).wait_send()

        for e in range(2):
            @pl.when(jnp.logical_not(is_self_m(e, t)))
            def _():
                out_m(e, t).wait_send()

    loop(0, runs, sent_out)


def shards(sensitivity, run_counts, req_owner, req_block, coupled):
    rows_dev, cols = sensitivity.shape
    blocks = run_counts.shape[0]
    nx, nz, nh, ny, nc = (lax.axis_size(a) for a in ("x", "zlo", "zhi", "y", "core"))
    regions = nx * nz
    runs = nh * ny * nc
    sub = [n * rows_dev // (nz * sum(PARTS)) for n in PARTS]
    vmem = pl.BlockSpec(memory_space=pltpu.VMEM)
    dma = pltpu.SemaphoreType.DMA

    fields = jnp.concatenate([req_block[:, None], coupled], axis=1)
    hit = req_owner[:, 0][:, None] == jnp.arange(regions, dtype=jnp.int32)[None, :]
    sorted_fields = jnp.sum(jnp.where(hit[:, None, :], fields[:, :, None], 0), axis=0)
    table = jnp.pad(sorted_fields, ((0, 8 - 1 - COUPLE), (0, 128 - regions)))

    acc = pl.pallas_call(
        functools.partial(gather_kernel, (nx, nz, ny, nc)),
        out_shape=jax.ShapeDtypeStruct((regions, COUPLE * BS, BS), jnp.float32),
        in_specs=[vmem, pl.BlockSpec(memory_space=pltpu.SMEM), vmem],
        out_specs=vmem,
        scratch_shapes=[
            pltpu.VMEM((nz, 8, 128), jnp.int32),
            pltpu.VMEM((nx, nz, 8, 128), jnp.int32),
            pltpu.SMEM((nx, nz, 8, 128), jnp.int32),
            dma((SPLIT, nz)), dma((SPLIT, nz)),
            dma((SPLIT, nz)), dma((SPLIT, nz)),
            dma((SPLIT, regions)), dma((SPLIT, regions)),
            dma((nz,)), dma((nz,)), dma((nx,)), dma((nx,)), dma,
        ] + [
            pltpu.VMEM(shape, jnp.bfloat16)
            for shape in (
                [(nz, blocks, n, BS) for n in sub] * 2
                + [(blocks, nz, n, BS) for n in sub]
                + [(blocks, BS, nz * n) for n in sub]
                + [(regions, nz * n, BS) for n in sub] * 2)
        ],
        compiler_params=pltpu.CompilerParams(
            collective_id=0, has_side_effects=True, vmem_limit_bytes=48 << 20),
    )(sensitivity, run_counts, table)

    share = BS // runs
    depth = nh * nz
    by_owner, by_source = pl.pallas_call(
        functools.partial(reduce_kernel, (nx, nz, nh, ny, nc)),
        out_shape=[jax.ShapeDtypeStruct((regions, COUPLE * share, BS), jnp.bfloat16)] * 2,
        in_specs=[vmem],
        out_specs=[vmem, vmem],
        scratch_shapes=[
            pltpu.VMEM((2, depth // 2, 2, COUPLE * BS, BS), jnp.float32),
            pltpu.VMEM((runs, 2, COUPLE * share, BS), jnp.bfloat16),
            dma((2, depth // 2, PIECES)), dma((2, depth // 2, PIECES)),
            dma((runs,)), dma((depth,)),
            dma((2, runs)), dma((regions,)),
        ],
        compiler_params=pltpu.CompilerParams(
            collective_id=1, has_side_effects=True, vmem_limit_bytes=32 << 20),
    )(acc)

    fisher = jnp.take(by_owner, req_owner[:, 0], axis=0).reshape(-1, COUPLE, share, BS)
    mirror = jnp.swapaxes(by_source.reshape(-1, COUPLE, share, BS), 2, 3)
    return fisher, mirror.reshape(1, regions, 1, COUPLE, BS, share)


def solution(mesh):
    fine = Mesh(mesh.devices.reshape(4, 8, 2, 4, 2), ("x", "zlo", "zhi", "y", "core"))
    return build(fine)


def build(fine):
    in_specs = (P(RUN, REGION), P(REGION), P(REGION, None), P(REGION), P(REGION, None))
    out_specs = (P(REGION, None, RUN, None), P(REGION, None, None, None, None, RUN))
    return jax.shard_map(shards, mesh=fine, in_specs=in_specs, out_specs=out_specs, check_vma=False)
```

```python
import functools

import jax
import jax.numpy as jnp
from jax import lax
from jax.experimental import pallas as pl
from jax.experimental.pallas import tpu as pltpu
from jax.sharding import Mesh, PartitionSpec as P

OBS = 4
COUPLE = 2
BS = 128
PARTS = (2, 1, 1, 1, 1)
SPLIT = len(PARTS)
PIECES = 8
REGION = ("x", "zlo")
RUN = ("zhi", "y", "core")
MESH = pl.DeviceIdType.MESH


def remote(src, dst, send, recv, where):
    return pltpu.make_async_remote_copy(
        src_ref=src, dst_ref=dst, send_sem=send, recv_sem=recv, device_id=where, device_id_type=MESH
    )


def loop(low, high, body):
    def step(i, carry):
        body(i)
        return carry

    lax.fori_loop(low, high, step, 0)


def reduction(sizes, barrier, acc, fbuf, mbuf, ring, fin, rs, rr, fs, fr, ms, mr):
    nx, nz, nh, ny, nc = sizes
    x, zlo, zhi = lax.axis_index("x"), lax.axis_index("zlo"), lax.axis_index("zhi")
    y, core = lax.axis_index("y"), lax.axis_index("core")
    rho = y * nc + core
    plane = x * nz + rho
    region = x * nz + zlo
    planes = nx * nz
    runs = nh * ny * nc
    mine = zhi * nz + rho
    depth = nh * nz
    z = zhi * nz + zlo
    ahead = [depth // 2, depth - 1 - depth // 2]
    pieces = [(e, h) for h in range(PIECES // 2) for e in range(2)]
    part = acc.shape[1] // (PIECES // 2)

    def z_of(k):
        return {"zhi": k // nz, "zlo": lax.rem(k, nz)}

    def run_of(t):
        r = lax.rem(t, nz)
        return {"zhi": t // nz, "y": r // nc, "core": lax.rem(r, nc)}

    def next_to(way):
        return z_of(lax.rem(z + (1 if way == 0 else depth - 1), depth))

    def fisher_to(t):
        return {"x": x, "zlo": rho, **run_of(t)}

    def mirror_to(e, t):
        q = 2 * z + e
        return {"x": q // nz, "zlo": lax.rem(q, nz), **run_of(t)}

    def fisher_from(k):
        return {"x": x, "y": zlo // nc, "core": lax.rem(zlo, nc), **z_of(k)}

    def mirror_from(s):
        r = lax.rem(s, nz)
        return {"x": s // nz, "y": r // nc, "core": lax.rem(r, nc), **z_of(region // 2)}

    fisher_self = zlo == rho
    mirror_self = z == region // 2

    def greet(where):
        pl.semaphore_signal(barrier, inc=1, device_id=where, device_id_type=MESH)

    def greet_fisher(k):
        @pl.when(jnp.logical_not(fisher_self & (k == z)))
        def _():
            greet(fisher_from(k))

    def greet_mirror(s):
        @pl.when(jnp.logical_not(mirror_self & (s == plane)))
        def _():
            greet(mirror_from(s))

    def greet_all():
        greet(next_to(0))
        greet(next_to(1))
        loop(0, depth, greet_fisher)
        loop(0, planes, greet_mirror)

    greeted = 2 + runs + 2 * runs - fisher_self.astype(jnp.int32) - mirror_self.astype(jnp.int32)

    def rows(h):
        return pl.ds(h * part, part)

    def chunk(way, i):
        if way == 0:
            return lax.rem(z + depth - 1 + ahead[0] - i, depth)
        return lax.rem(z + depth + 1 - ahead[1] + i, depth)

    def hop(way, i, p, src):
        e, h = pieces[p]
        return remote(
            src, ring.at[way, i, e, rows(h)], rs.at[way, i, p], rr.at[way, i, p], next_to(way))

    def first(way, p):
        e, h = pieces[p]
        own = lax.rem(z + depth + (ahead[0] if way == 0 else -ahead[1]), depth)
        return hop(way, 0, p, acc.at[2 * own + e, rows(h)])

    def later(way, i, p):
        e, h = pieces[p]
        return hop(way, i + 1, p, ring.at[way, i, e, rows(h)])

    def arrive(way, i, p):
        e, h = pieces[p]
        dst = ring.at[way, i, e, rows(h)]
        pltpu.make_async_copy(dst, dst, rr.at[way, i, p]).wait()

    def step(i, ways):
        for p, (e, h) in enumerate(pieces):
            for way in ways:
                arrive(way, i, p)
                ring[way, i, e, rows(h)] += acc[2 * chunk(way, i) + e, rows(h)]
                later(way, i, p).start()

    ways = [way for way in range(2) if ahead[way] > 0]
    both = max(0, ahead[1] - 1)
    def run():
        for p in range(len(pieces)):
            for way in ways:
                first(way, p).start()
        loop(0, both, lambda i: step(i, [0, 1]))
        for i in range(both, ahead[0] - 1):
            step(i, [0])
        for way in ways:
            for p in range(len(pieces)):
                arrive(way, ahead[way] - 1, p)
        for e in range(2):
            total = acc[2 * z + e]
            for way in ways:
                total += ring[way, ahead[way] - 1, e]
            slices = total.reshape(COUPLE, runs, BS // runs, BS)
            fin[:, e] = jnp.concatenate([slices[c] for c in range(COUPLE)], axis=1).astype(jnp.bfloat16)

        def out_f(t):
            return remote(fin.at[t], fbuf.at[pl.ds(2 * z, 2)], fs.at[t], fr.at[z], fisher_to(t))

        def out_m(e, t):
            return remote(fin.at[t, e], mbuf.at[plane], ms.at[e, t], mr.at[plane], mirror_to(e, t))

        def self_f():
            return pltpu.make_async_copy(fin.at[mine], fbuf.at[pl.ds(2 * z, 2)], fr.at[z])

        def self_m():
            return pltpu.make_async_copy(
                fin.at[mine, lax.rem(region, 2)], mbuf.at[plane], mr.at[plane])

        def is_self_m(e, t):
            return (2 * z + e == region) & (t == mine)

        def send(k):
            t = lax.rem(mine + k, runs)

            @pl.when(jnp.logical_not(fisher_self & (t == mine)))
            def _():
                out_f(t).start()

            for e in range(2):
                @pl.when(jnp.logical_not(is_self_m(e, t)))
                def _():
                    out_m(e, t).start()

        loop(0, runs, send)

        @pl.when(fisher_self)
        def _():
            self_f().start()

        @pl.when(mirror_self)
        def _():
            self_m().start()

        def got_f(k):
            dst = fbuf.at[pl.ds(2 * k, 2)]
            pltpu.make_async_copy(dst, dst, fr.at[k]).wait()

        def got_m(s):
            dst = mbuf.at[s]
            pltpu.make_async_copy(dst, dst, mr.at[s]).wait()

        loop(0, depth, got_f)
        loop(0, planes, got_m)

        for p in range(len(pieces)):
            for way in ways:
                first(way, p).wait_send()

        def sent(way, i):
            for p in range(len(pieces)):
                later(way, i, p).wait_send()

        for way in ways:
            loop(0, ahead[way] - 1, functools.partial(sent, way))

        def sent_out(t):
            @pl.when(jnp.logical_not(fisher_self & (t == mine)))
            def _():
                out_f(t).wait_send()

            for e in range(2):
                @pl.when(jnp.logical_not(is_self_m(e, t)))
                def _():
                    out_m(e, t).wait_send()

        loop(0, runs, sent_out)

    return greet_all, greeted, run


def fisher_kernel(
    sizes, sens, counts, table, fbuf, mbuf, acc, ring, fin, rs, rr, fs, fr, ms, mr,
    ztab, xtab, stab, zs, zr, ys, yr, ps, pr, tzs, tzr, txs, txr, tsem, *bufs,
):
    masked, zbufs, tbufs, turned, outbufs, inbufs = (
        bufs[i * SPLIT:(i + 1) * SPLIT] for i in range(6))
    nx, nz, nh, ny, nc = sizes
    x, zlo = lax.axis_index("x"), lax.axis_index("zlo")
    y, core = lax.axis_index("y"), lax.axis_index("core")
    rho = y * nc + core
    plane = x * nz + rho
    planes = nx * nz
    stride = 11 % planes
    blocks = masked[0].shape[1]
    sub = [m.shape[2] for m in masked]
    offset = [sum(sub[:s]) for s in range(SPLIT)]
    first_run = (lax.axis_index("zhi") * nz + rho) * (sens.shape[0] // OBS)

    def z_at(d):
        return {"zlo": lax.rem(zlo + d, nz)}

    def yc_at(t):
        return {"y": t // nc, "core": lax.rem(t, nc)}

    def x_at(d):
        return {"x": lax.rem(x + d, nx)}

    def plane_at(t):
        r = lax.rem(t, nz)
        return {"x": t // nz, "y": r // nc, "core": lax.rem(r, nc)}

    barrier = pltpu.get_barrier_semaphore()
    greet_all, greeted, reduce_over_z = reduction(
        sizes, barrier, acc, fbuf, mbuf, ring, fin, rs, rr, fs, fr, ms, mr)
    greet_all()
    loop(1, nz, lambda d: pl.semaphore_signal(barrier, inc=1, device_id=z_at(d), device_id_type=MESH))
    loop(1, planes, lambda g: pl.semaphore_signal(
        barrier, inc=1, device_id=plane_at(lax.rem(plane + g, planes)), device_id_type=MESH))

    def table_copy(d):
        return remote(table, ztab.at[zlo], tzs.at[d], tzr.at[d], z_at(d))

    def row_copy(x_from, d):
        return remote(ztab, xtab.at[x_from], txs.at[d], txr.at[d], x_at(d))

    def z_copy(s, d):
        return remote(
            masked[s].at[lax.rem(zlo + d, nz)], zbufs[s].at[zlo], zs.at[s, d], zr.at[s, d], z_at(d))

    def y_copy(s, e):
        t = lax.rem(rho + e, nz)
        return remote(zbufs[s].at[t], tbufs[s].at[:, rho], ys.at[s, e], yr.at[s, e], yc_at(t))

    def p_copy(s, g):
        return remote(
            outbufs[s].at[g], inbufs[s].at[plane], ps.at[s, g], pr.at[s, g],
            plane_at(lax.rem(plane + g, planes)))

    def mask(j, s):
        start = pl.multiple_of(j * sum(sub) + offset[s], sub[-1])
        run = (start + lax.broadcasted_iota(jnp.int32, (sub[s], BS), 0)) // OBS + first_run
        for b in range(blocks):
            value = sens[pl.ds(start, sub[s]), b * BS:(b + 1) * BS].astype(jnp.float32)
            masked[s][j, b] = jnp.where(run < counts[b], value, 0.0).astype(jnp.bfloat16)

    early = min(nz // 2, nz - 1)

    def z_self(s):
        mask(zlo, s)
        pltpu.make_async_copy(masked[s].at[zlo], zbufs[s].at[zlo], zr.at[s, 0]).start()

    def z_one(s, i):
        d = lax.rem(i * 3, nz)
        mask(lax.rem(zlo + d, nz), s)
        z_copy(s, d).start()

    def z_wait(s, d):
        dst = zbufs[s].at[lax.rem(zlo + nz - d, nz)]
        pltpu.make_async_copy(dst, dst, zr.at[s, d]).wait()

    def relay(s):
        def one(i):
            d = lax.rem(i * 3, nz)
            z_wait(s, d)
            e = lax.rem(zlo + 2 * nz - d - rho, nz)

            @pl.when(e == 0)
            def _():
                pltpu.make_async_copy(zbufs[s].at[rho], tbufs[s].at[:, rho], yr.at[s, 0]).start()

            @pl.when(e > 0)
            def _():
                y_copy(s, e).start()

        if s + 1 < SPLIT:
            def both(i):
                one(i)
                z_one(s + 1, i + 1)

            loop(0, early, both)
            loop(early, nz, one)
            z_self(s + 1)
        else:
            loop(0, nz, one)

    def block(s, b):
        return tbufs[s][b].reshape(nz * sub[s], BS)

    def asked(t):
        return stab[t // nz, lax.rem(t, nz), 0, plane]

    def pick(s):
        def ready(e):
            dst = tbufs[s].at[:, lax.rem(rho + nz - e, nz)]
            pltpu.make_async_copy(dst, dst, yr.at[s, e]).wait()

        loop(0, nz, ready)

        def one(i):
            g = lax.rem(i * stride, planes)
            outbufs[s][g] = block(s, asked(lax.rem(plane + g, planes)))
            p_copy(s, g).start()

        groups = nz - 1 - early if s + 1 < SPLIT else 0
        begin = 1
        for j in range(groups):
            end = 1 + (planes - 1) * (j + 1) // (groups + 1)
            loop(begin, end, one)
            z_one(s + 1, early + 1 + j)
            begin = end
        loop(begin, planes, one)
        inbufs[s][plane] = block(s, asked(plane))

    def turn(s):
        def one(b):
            turned[s][b] = tbufs[s][b].reshape(nz * sub[s], BS).T

        loop(0, blocks, one)

    def multiply(s):
        def product(q):
            near = jnp.concatenate(
                [turned[s][stab[x, rho, 1 + c, q]] for c in range(COUPLE)], axis=0)
            value = jnp.dot(near, inbufs[s][q], preferred_element_type=jnp.float32)
            if s == 0:
                acc[q] = value
            else:
                acc[q] += value

        def one(i):
            g = lax.rem(i * stride, planes)
            q = lax.rem(plane + planes - g, planes)
            dst = inbufs[s].at[q]
            pltpu.make_async_copy(dst, dst, pr.at[s, g]).wait()
            product(q)

        product(plane)
        loop(1, planes, one)

    pl.semaphore_wait(barrier, nz - 1 + planes - 1 + greeted)

    pltpu.make_async_copy(table, ztab.at[zlo], tzr.at[0]).start()
    loop(1, nz, lambda d: table_copy(d).start())
    loop(1, nz, lambda i: z_one(0, i))
    z_self(0)

    def table_wait(d):
        dst = ztab.at[lax.rem(zlo + nz - d, nz)]
        pltpu.make_async_copy(dst, dst, tzr.at[d]).wait()

    loop(0, nz, table_wait)
    pltpu.make_async_copy(ztab, xtab.at[x], txr.at[0]).start()
    loop(1, nx, lambda d: row_copy(x, d).start())

    for s in range(SPLIT):
        relay(s)
        if s == 0:
            def row_wait(d):
                dst = xtab.at[lax.rem(x + nx - d, nx)]
                pltpu.make_async_copy(dst, dst, txr.at[d]).wait()

            loop(0, nx, row_wait)
            fetch = pltpu.make_async_copy(xtab, stab, tsem)
            fetch.start()
            fetch.wait()
        pick(s)
        if s > 0:
            multiply(s - 1)
        turn(s)
    multiply(SPLIT - 1)
    reduce_over_z()

    loop(1, nz, lambda d: table_copy(d).wait_send())
    loop(1, nx, lambda d: row_copy(x, d).wait_send())
    for s in range(SPLIT):
        loop(1, nz, lambda d: z_copy(s, d).wait_send())
        loop(1, nz, lambda e: y_copy(s, e).wait_send())
        loop(1, planes, lambda g: p_copy(s, g).wait_send())


def shards(sensitivity, run_counts, req_owner, req_block, coupled):
    rows_dev, cols = sensitivity.shape
    blocks = run_counts.shape[0]
    nx, nz, nh, ny, nc = (lax.axis_size(a) for a in ("x", "zlo", "zhi", "y", "core"))
    regions = nx * nz
    runs = nh * ny * nc
    sub = [n * rows_dev // (nz * sum(PARTS)) for n in PARTS]
    vmem = pl.BlockSpec(memory_space=pltpu.VMEM)
    dma = pltpu.SemaphoreType.DMA

    fields = jnp.concatenate([req_block[:, None], coupled], axis=1)
    hit = req_owner[:, 0][:, None] == jnp.arange(regions, dtype=jnp.int32)[None, :]
    sorted_fields = jnp.sum(jnp.where(hit[:, None, :], fields[:, :, None], 0), axis=0)
    table = jnp.pad(sorted_fields, ((0, 8 - 1 - COUPLE), (0, 128 - regions)))

    share = BS // runs
    depth = nh * nz
    by_owner, by_source = pl.pallas_call(
        functools.partial(fisher_kernel, (nx, nz, nh, ny, nc)),
        out_shape=[jax.ShapeDtypeStruct((regions, COUPLE * share, BS), jnp.bfloat16)] * 2,
        in_specs=[vmem, pl.BlockSpec(memory_space=pltpu.SMEM), vmem],
        out_specs=[vmem, vmem],
        scratch_shapes=[
            pltpu.VMEM((regions, COUPLE * BS, BS), jnp.float32),
            pltpu.VMEM((2, depth // 2, 2, COUPLE * BS, BS), jnp.float32),
            pltpu.VMEM((runs, 2, COUPLE * share, BS), jnp.bfloat16),
            dma((2, depth // 2, PIECES)), dma((2, depth // 2, PIECES)),
            dma((runs,)), dma((depth,)),
            dma((2, runs)), dma((regions,)),
            pltpu.VMEM((nz, 8, 128), jnp.int32),
            pltpu.VMEM((nx, nz, 8, 128), jnp.int32),
            pltpu.SMEM((nx, nz, 8, 128), jnp.int32),
            dma((SPLIT, nz)), dma((SPLIT, nz)),
            dma((SPLIT, nz)), dma((SPLIT, nz)),
            dma((SPLIT, regions)), dma((SPLIT, regions)),
            dma((nz,)), dma((nz,)), dma((nx,)), dma((nx,)), dma,
        ] + [
            pltpu.VMEM(shape, jnp.bfloat16)
            for shape in (
                [(nz, blocks, n, BS) for n in sub] * 2
                + [(blocks, nz, n, BS) for n in sub]
                + [(blocks, BS, nz * n) for n in sub]
                + [(regions, nz * n, BS) for n in sub] * 2)
        ],
        compiler_params=pltpu.CompilerParams(
            collective_id=0, has_side_effects=True, vmem_limit_bytes=54 << 20),
    )(sensitivity, run_counts, table)

    fisher = jnp.take(by_owner, req_owner[:, 0], axis=0).reshape(-1, COUPLE, share, BS)
    mirror = jnp.swapaxes(by_source.reshape(-1, COUPLE, share, BS), 2, 3)
    return fisher, mirror.reshape(1, regions, 1, COUPLE, BS, share)


def solution(mesh):
    fine = Mesh(mesh.devices.reshape(4, 8, 2, 4, 2), ("x", "zlo", "zhi", "y", "core"))
    return build(fine)


def build(fine):
    in_specs = (P(RUN, REGION), P(REGION), P(REGION, None), P(REGION), P(REGION, None))
    out_specs = (P(REGION, None, RUN, None), P(REGION, None, None, None, None, RUN))
    return jax.shard_map(shards, mesh=fine, in_specs=in_specs, out_specs=out_specs, check_vma=False)
```

```python
import functools

import jax
import jax.numpy as jnp
from jax import lax
from jax.experimental import pallas as pl
from jax.experimental.pallas import tpu as pltpu
from jax.sharding import Mesh, PartitionSpec as P

OBS = 4
COUPLE = 2
BS = 128
PARTS = (2, 1, 1, 1, 1)
SPLIT = len(PARTS)
PIECES = 8
REGION = ("x", "zlo")
RUN = ("zhi", "y", "core")
MESH = pl.DeviceIdType.MESH


def remote(src, dst, send, recv, where):
    return pltpu.make_async_remote_copy(
        src_ref=src, dst_ref=dst, send_sem=send, recv_sem=recv, device_id=where, device_id_type=MESH
    )


def loop(low, high, body):
    def step(i, carry):
        body(i)
        return carry

    lax.fori_loop(low, high, step, 0)


def reduction(sizes, barrier, acc, fbuf, mbuf, ring, fin, rs, rr, fs, fr, ms, mr):
    nx, nz, nh, ny, nc = sizes
    x, zlo, zhi = lax.axis_index("x"), lax.axis_index("zlo"), lax.axis_index("zhi")
    y, core = lax.axis_index("y"), lax.axis_index("core")
    rho = y * nc + core
    plane = x * nz + rho
    region = x * nz + zlo
    planes = nx * nz
    runs = nh * ny * nc
    mine = zhi * nz + rho
    depth = nh * nz
    z = zhi * nz + zlo
    ahead = [depth // 2, depth - 1 - depth // 2]
    pieces = [(e, h) for h in range(PIECES // 2) for e in range(2)]
    part = acc.shape[1] // (PIECES // 2)

    def z_of(k):
        return {"zhi": k // nz, "zlo": lax.rem(k, nz)}

    def run_of(t):
        r = lax.rem(t, nz)
        return {"zhi": t // nz, "y": r // nc, "core": lax.rem(r, nc)}

    def next_to(way):
        return z_of(lax.rem(z + (1 if way == 0 else depth - 1), depth))

    def fisher_to(t):
        return {"x": x, "zlo": rho, **run_of(t)}

    def mirror_to(e, t):
        q = 2 * z + e
        return {"x": q // nz, "zlo": lax.rem(q, nz), **run_of(t)}

    def fisher_from(k):
        return {"x": x, "y": zlo // nc, "core": lax.rem(zlo, nc), **z_of(k)}

    def mirror_from(s):
        r = lax.rem(s, nz)
        return {"x": s // nz, "y": r // nc, "core": lax.rem(r, nc), **z_of(region // 2)}

    fisher_self = zlo == rho
    mirror_self = z == region // 2

    def greet(where):
        pl.semaphore_signal(barrier, inc=1, device_id=where, device_id_type=MESH)

    def greet_fisher(k):
        @pl.when(jnp.logical_not(fisher_self & (k == z)))
        def _():
            greet(fisher_from(k))

    def greet_mirror(s):
        @pl.when(jnp.logical_not(mirror_self & (s == plane)))
        def _():
            greet(mirror_from(s))

    def greet_all():
        greet(next_to(0))
        greet(next_to(1))
        loop(0, depth, greet_fisher)
        loop(0, planes, greet_mirror)

    greeted = 2 + runs + 2 * runs - fisher_self.astype(jnp.int32) - mirror_self.astype(jnp.int32)

    def rows(h):
        return pl.ds(h * part, part)

    def chunk(way, i):
        if way == 0:
            return lax.rem(z + depth - 1 + ahead[0] - i, depth)
        return lax.rem(z + depth + 1 - ahead[1] + i, depth)

    def hop(way, i, p, src):
        e, h = pieces[p]
        return remote(
            src, ring.at[way, i, e, rows(h)], rs.at[way, i, p], rr.at[way, i, p], next_to(way))

    def first(way, p):
        e, h = pieces[p]
        own = lax.rem(z + depth + (ahead[0] if way == 0 else -ahead[1]), depth)
        return hop(way, 0, p, acc.at[2 * own + e, rows(h)])

    def later(way, i, p):
        e, h = pieces[p]
        return hop(way, i + 1, p, ring.at[way, i, e, rows(h)])

    def arrive(way, i, p):
        e, h = pieces[p]
        dst = ring.at[way, i, e, rows(h)]
        pltpu.make_async_copy(dst, dst, rr.at[way, i, p]).wait()

    def step(i, ways):
        for p, (e, h) in enumerate(pieces):
            for way in ways:
                arrive(way, i, p)
                ring[way, i, e, rows(h)] += acc[2 * chunk(way, i) + e, rows(h)]
                later(way, i, p).start()

    ways = [way for way in range(2) if ahead[way] > 0]
    both = max(0, ahead[1] - 1)
    def run(finish):
        def complete(b):
            for e in range(2):
                finish(2 * b + e)

        def start_of(way):
            return lax.rem(z + depth + (ahead[0] if way == 0 else -ahead[1]), depth)

        for way in ways:
            complete(start_of(way))
            for p in range(len(pieces)):
                first(way, p).start()
        def next_step(i, ways):
            for way in ways:
                complete(chunk(way, i))
            step(i, ways)

        loop(0, both, lambda i: next_step(i, [0, 1]))
        for i in range(both, ahead[0] - 1):
            next_step(i, [0])
        complete(z)
        for way in ways:
            for p in range(len(pieces)):
                arrive(way, ahead[way] - 1, p)
        for e in range(2):
            total = acc[2 * z + e]
            for way in ways:
                total += ring[way, ahead[way] - 1, e]
            slices = total.reshape(COUPLE, runs, BS // runs, BS)
            fin[:, e] = jnp.concatenate([slices[c] for c in range(COUPLE)], axis=1).astype(jnp.bfloat16)

        def out_f(t):
            return remote(fin.at[t], fbuf.at[pl.ds(2 * z, 2)], fs.at[t], fr.at[z], fisher_to(t))

        def out_m(e, t):
            return remote(fin.at[t, e], mbuf.at[plane], ms.at[e, t], mr.at[plane], mirror_to(e, t))

        def self_f():
            return pltpu.make_async_copy(fin.at[mine], fbuf.at[pl.ds(2 * z, 2)], fr.at[z])

        def self_m():
            return pltpu.make_async_copy(
                fin.at[mine, lax.rem(region, 2)], mbuf.at[plane], mr.at[plane])

        def is_self_m(e, t):
            return (2 * z + e == region) & (t == mine)

        def send(k):
            t = lax.rem(mine + k, runs)

            @pl.when(jnp.logical_not(fisher_self & (t == mine)))
            def _():
                out_f(t).start()

            for e in range(2):
                @pl.when(jnp.logical_not(is_self_m(e, t)))
                def _():
                    out_m(e, t).start()

        loop(0, runs, send)

        @pl.when(fisher_self)
        def _():
            self_f().start()

        @pl.when(mirror_self)
        def _():
            self_m().start()

        def got_f(k):
            dst = fbuf.at[pl.ds(2 * k, 2)]
            pltpu.make_async_copy(dst, dst, fr.at[k]).wait()

        def got_m(s):
            dst = mbuf.at[s]
            pltpu.make_async_copy(dst, dst, mr.at[s]).wait()

        loop(0, depth, got_f)
        loop(0, planes, got_m)

        for p in range(len(pieces)):
            for way in ways:
                first(way, p).wait_send()

        def sent(way, i):
            for p in range(len(pieces)):
                later(way, i, p).wait_send()

        for way in ways:
            loop(0, ahead[way] - 1, functools.partial(sent, way))

        def sent_out(t):
            @pl.when(jnp.logical_not(fisher_self & (t == mine)))
            def _():
                out_f(t).wait_send()

            for e in range(2):
                @pl.when(jnp.logical_not(is_self_m(e, t)))
                def _():
                    out_m(e, t).wait_send()

        loop(0, runs, sent_out)

    return greet_all, greeted, run


def fisher_kernel(
    sizes, shard, counts, table, fbuf, mbuf, acc, ring, fin, rs, rr, fs, fr, ms, mr,
    sens, ztab, xtab, stab, zs, zr, ys, yr, ps, pr, tzs, tzr, txs, txr, tsem, *bufs,
):
    masked, zbufs, tbufs, turned, outbufs, inbufs = (
        bufs[i * SPLIT:(i + 1) * SPLIT] for i in range(6))
    nx, nz, nh, ny, nc = sizes
    x, zlo = lax.axis_index("x"), lax.axis_index("zlo")
    y, core = lax.axis_index("y"), lax.axis_index("core")
    rho = y * nc + core
    plane = x * nz + rho
    planes = nx * nz
    stride = 11 % planes
    blocks = masked[0].shape[1]
    sub = [m.shape[2] for m in masked]
    offset = [sum(sub[:s]) for s in range(SPLIT)]
    first_run = (lax.axis_index("zhi") * nz + rho) * (sens.shape[0] // OBS)

    def z_at(d):
        return {"zlo": lax.rem(zlo + d, nz)}

    def yc_at(t):
        return {"y": t // nc, "core": lax.rem(t, nc)}

    def x_at(d):
        return {"x": lax.rem(x + d, nx)}

    def plane_at(t):
        r = lax.rem(t, nz)
        return {"x": t // nz, "y": r // nc, "core": lax.rem(r, nc)}

    barrier = pltpu.get_barrier_semaphore()
    greet_all, greeted, reduce_over_z = reduction(
        sizes, barrier, acc, fbuf, mbuf, ring, fin, rs, rr, fs, fr, ms, mr)
    load = pltpu.make_async_copy(shard, sens, tsem)
    load.start()
    greet_all()
    loop(1, nz, lambda d: pl.semaphore_signal(barrier, inc=1, device_id=z_at(d), device_id_type=MESH))
    loop(1, planes, lambda g: pl.semaphore_signal(
        barrier, inc=1, device_id=plane_at(lax.rem(plane + g, planes)), device_id_type=MESH))

    def table_copy(d):
        return remote(table, ztab.at[zlo], tzs.at[d], tzr.at[d], z_at(d))

    def row_copy(x_from, d):
        return remote(ztab, xtab.at[x_from], txs.at[d], txr.at[d], x_at(d))

    def z_copy(s, d):
        return remote(
            masked[s].at[lax.rem(zlo + d, nz)], zbufs[s].at[zlo], zs.at[s, d], zr.at[s, d], z_at(d))

    def y_copy(s, e):
        t = lax.rem(rho + e, nz)
        return remote(zbufs[s].at[t], tbufs[s].at[:, rho], ys.at[s, e], yr.at[s, e], yc_at(t))

    def p_copy(s, g):
        return remote(
            outbufs[s].at[g], inbufs[s].at[plane], ps.at[s, g], pr.at[s, g],
            plane_at(lax.rem(plane + g, planes)))

    def mask(j, s):
        start = pl.multiple_of(j * sum(sub) + offset[s], sub[-1])
        run = (start + lax.broadcasted_iota(jnp.int32, (sub[s], BS), 0)) // OBS + first_run
        for b in range(blocks):
            value = sens[pl.ds(start, sub[s]), b * BS:(b + 1) * BS].astype(jnp.float32)
            masked[s][j, b] = jnp.where(run < counts[b], value, 0.0).astype(jnp.bfloat16)

    def z_self(s):
        mask(zlo, s)
        pltpu.make_async_copy(masked[s].at[zlo], zbufs[s].at[zlo], zr.at[s, 0]).start()

    def z_one(s, i):
        d = lax.rem(i * 3, nz)
        mask(lax.rem(zlo + d, nz), s)
        z_copy(s, d).start()

    def z_wait(s, d):
        dst = zbufs[s].at[lax.rem(zlo + nz - d, nz)]
        pltpu.make_async_copy(dst, dst, zr.at[s, d]).wait()

    def relay(s):
        def one(i):
            d = lax.rem(i * 3, nz)
            z_wait(s, d)
            e = lax.rem(zlo + 2 * nz - d - rho, nz)

            @pl.when(e == 0)
            def _():
                pltpu.make_async_copy(zbufs[s].at[rho], tbufs[s].at[:, rho], yr.at[s, 0]).start()

            @pl.when(e > 0)
            def _():
                y_copy(s, e).start()

        if s + 2 < SPLIT:
            def both(i):
                one(i)
                z_one(s + 2, i + 1)

            loop(0, nz - 1, both)
            one(nz - 1)
            z_self(s + 2)
        else:
            loop(0, nz, one)

    def block(s, b):
        return tbufs[s][b].reshape(nz * sub[s], BS)

    def asked(t):
        return stab[t // nz, lax.rem(t, nz), 0, plane]

    def pick(s):
        def ready(e):
            dst = tbufs[s].at[:, lax.rem(rho + nz - e, nz)]
            pltpu.make_async_copy(dst, dst, yr.at[s, e]).wait()

        loop(0, nz, ready)

        def one(i):
            g = lax.rem(i * stride, planes)
            outbufs[s][g] = block(s, asked(lax.rem(plane + g, planes)))
            p_copy(s, g).start()

        loop(1, planes, one)
        inbufs[s][plane] = block(s, asked(plane))

    def turn(s):
        def one(b):
            turned[s][b] = tbufs[s][b].reshape(nz * sub[s], BS).T

        loop(0, blocks, one)

    def product(s, q):
        g = lax.rem(plane + planes - q, planes)

        @pl.when(g > 0)
        def _():
            dst = inbufs[s].at[q]
            pltpu.make_async_copy(dst, dst, pr.at[s, g]).wait()

        near = jnp.concatenate(
            [turned[s][stab[x, rho, 1 + c, q]] for c in range(COUPLE)], axis=0)
        value = jnp.dot(near, inbufs[s][q], preferred_element_type=jnp.float32)
        if s == 0:
            acc[q] = value
        else:
            acc[q] += value

    def multiply(s):
        def one(i):
            g = lax.rem(i * stride, planes)
            product(s, lax.rem(plane + planes - g, planes))

        loop(0, planes, one)

    load.wait()
    pl.semaphore_wait(barrier, nz - 1 + planes - 1 + greeted)

    pltpu.make_async_copy(table, ztab.at[zlo], tzr.at[0]).start()
    loop(1, nz, lambda d: table_copy(d).start())
    for s in range(2):
        loop(1, nz, lambda i: z_one(s, i))
        z_self(s)

    def table_wait(d):
        dst = ztab.at[lax.rem(zlo + nz - d, nz)]
        pltpu.make_async_copy(dst, dst, tzr.at[d]).wait()

    loop(0, nz, table_wait)
    pltpu.make_async_copy(ztab, xtab.at[x], txr.at[0]).start()
    loop(1, nx, lambda d: row_copy(x, d).start())

    for s in range(SPLIT):
        relay(s)
        if s == 0:
            def row_wait(d):
                dst = xtab.at[lax.rem(x + nx - d, nx)]
                pltpu.make_async_copy(dst, dst, txr.at[d]).wait()

            loop(0, nx, row_wait)
            fetch = pltpu.make_async_copy(xtab, stab, tsem)
            fetch.start()
            fetch.wait()
        pick(s)
        if s > 0:
            multiply(s - 1)
        turn(s)
    reduce_over_z(functools.partial(product, SPLIT - 1))

    loop(1, nz, lambda d: table_copy(d).wait_send())
    loop(1, nx, lambda d: row_copy(x, d).wait_send())
    for s in range(SPLIT):
        loop(1, nz, lambda d: z_copy(s, d).wait_send())
        loop(1, nz, lambda e: y_copy(s, e).wait_send())
        loop(1, planes, lambda g: p_copy(s, g).wait_send())


def shards(sensitivity, run_counts, req_owner, req_block, coupled):
    rows_dev, cols = sensitivity.shape
    blocks = run_counts.shape[0]
    nx, nz, nh, ny, nc = (lax.axis_size(a) for a in ("x", "zlo", "zhi", "y", "core"))
    regions = nx * nz
    runs = nh * ny * nc
    sub = [n * rows_dev // (nz * sum(PARTS)) for n in PARTS]
    vmem = pl.BlockSpec(memory_space=pltpu.VMEM)
    dma = pltpu.SemaphoreType.DMA

    fields = jnp.concatenate([req_block[:, None], coupled], axis=1)
    hit = req_owner[:, 0][:, None] == jnp.arange(regions, dtype=jnp.int32)[None, :]
    sorted_fields = jnp.sum(jnp.where(hit[:, None, :], fields[:, :, None], 0), axis=0)
    table = jnp.pad(sorted_fields, ((0, 8 - 1 - COUPLE), (0, 128 - regions)))

    share = BS // runs
    depth = nh * nz
    by_owner, by_source = pl.pallas_call(
        functools.partial(fisher_kernel, (nx, nz, nh, ny, nc)),
        out_shape=[jax.ShapeDtypeStruct((regions, COUPLE * share, BS), jnp.bfloat16)] * 2,
        in_specs=[pl.BlockSpec(memory_space=pl.ANY), pl.BlockSpec(memory_space=pltpu.SMEM), vmem],
        out_specs=[vmem, vmem],
        scratch_shapes=[
            pltpu.VMEM((regions, COUPLE * BS, BS), jnp.float32),
            pltpu.VMEM((2, depth // 2, 2, COUPLE * BS, BS), jnp.float32),
            pltpu.VMEM((runs, 2, COUPLE * share, BS), jnp.bfloat16),
            dma((2, depth // 2, PIECES)), dma((2, depth // 2, PIECES)),
            dma((runs,)), dma((depth,)),
            dma((2, runs)), dma((regions,)),
            pltpu.VMEM((rows_dev, cols), jnp.bfloat16),
            pltpu.VMEM((nz, 8, 128), jnp.int32),
            pltpu.VMEM((nx, nz, 8, 128), jnp.int32),
            pltpu.SMEM((nx, nz, 8, 128), jnp.int32),
            dma((SPLIT, nz)), dma((SPLIT, nz)),
            dma((SPLIT, nz)), dma((SPLIT, nz)),
            dma((SPLIT, regions)), dma((SPLIT, regions)),
            dma((nz,)), dma((nz,)), dma((nx,)), dma((nx,)), dma,
        ] + [
            pltpu.VMEM(shape, jnp.bfloat16)
            for shape in (
                [(nz, blocks, n, BS) for n in sub] * 2
                + [(blocks, nz, n, BS) for n in sub]
                + [(blocks, BS, nz * n) for n in sub]
                + [(regions, nz * n, BS) for n in sub] * 2)
        ],
        compiler_params=pltpu.CompilerParams(
            collective_id=0, has_side_effects=True, vmem_limit_bytes=54 << 20),
    )(sensitivity, run_counts, table)

    fisher = jnp.take(by_owner, req_owner[:, 0], axis=0).reshape(-1, COUPLE, share, BS)
    mirror = jnp.swapaxes(by_source.reshape(-1, COUPLE, share, BS), 2, 3)
    return fisher, mirror.reshape(1, regions, 1, COUPLE, BS, share)


def solution(mesh):
    fine = Mesh(mesh.devices.reshape(4, 8, 2, 4, 2), ("x", "zlo", "zhi", "y", "core"))
    return build(fine)


def build(fine):
    in_specs = (P(RUN, REGION), P(REGION), P(REGION, None), P(REGION), P(REGION, None))
    out_specs = (P(REGION, None, RUN, None), P(REGION, None, None, None, None, RUN))
    return jax.shard_map(shards, mesh=fine, in_specs=in_specs, out_specs=out_specs, check_vma=False)
```

```python
import functools

import jax
import jax.numpy as jnp
from jax import lax
from jax.experimental import pallas as pl
from jax.experimental.pallas import tpu as pltpu
from jax.sharding import Mesh, PartitionSpec as P

OBS = 4
COUPLE = 2
BS = 128
PARTS = (2, 1, 1, 1, 1)
SPLIT = len(PARTS)
PIECES = 8
REGION = ("x", "zlo")
RUN = ("zhi", "y", "core")
MESH = pl.DeviceIdType.MESH


def remote(src, dst, send, recv, where):
    return pltpu.make_async_remote_copy(
        src_ref=src, dst_ref=dst, send_sem=send, recv_sem=recv, device_id=where, device_id_type=MESH
    )


def loop(low, high, body):
    def step(i, carry):
        body(i)
        return carry

    lax.fori_loop(low, high, step, 0)


def reduction(sizes, barrier, acc, fbuf, mbuf, ring, fin, rs, rr, fs, fr, ms, mr):
    nx, nz, nh, ny, nc = sizes
    x, zlo, zhi = lax.axis_index("x"), lax.axis_index("zlo"), lax.axis_index("zhi")
    y, core = lax.axis_index("y"), lax.axis_index("core")
    rho = y * nc + core
    plane = x * nz + rho
    region = x * nz + zlo
    planes = nx * nz
    runs = nh * ny * nc
    mine = zhi * nz + rho
    depth = nh * nz
    z = zhi * nz + zlo
    ahead = [depth // 2, depth - 1 - depth // 2]
    pieces = [(e, h) for h in range(PIECES // 2) for e in range(2)]
    part = acc.shape[1] // (PIECES // 2)

    def z_of(k):
        return {"zhi": k // nz, "zlo": lax.rem(k, nz)}

    def run_of(t):
        r = lax.rem(t, nz)
        return {"zhi": t // nz, "y": r // nc, "core": lax.rem(r, nc)}

    def next_to(way):
        return z_of(lax.rem(z + (1 if way == 0 else depth - 1), depth))

    def fisher_to(t):
        return {"x": x, "zlo": rho, **run_of(t)}

    def mirror_to(e, t):
        q = 2 * z + e
        return {"x": q // nz, "zlo": lax.rem(q, nz), **run_of(t)}

    def fisher_from(k):
        return {"x": x, "y": zlo // nc, "core": lax.rem(zlo, nc), **z_of(k)}

    def mirror_from(s):
        r = lax.rem(s, nz)
        return {"x": s // nz, "y": r // nc, "core": lax.rem(r, nc), **z_of(region // 2)}

    fisher_self = zlo == rho
    mirror_self = z == region // 2

    def greet(where):
        pl.semaphore_signal(barrier, inc=1, device_id=where, device_id_type=MESH)

    def greet_fisher(k):
        @pl.when(jnp.logical_not(fisher_self & (k == z)))
        def _():
            greet(fisher_from(k))

    def greet_mirror(s):
        @pl.when(jnp.logical_not(mirror_self & (s == plane)))
        def _():
            greet(mirror_from(s))

    def greet_all():
        greet(next_to(0))
        greet(next_to(1))
        loop(0, depth, greet_fisher)
        loop(0, planes, greet_mirror)

    greeted = 2 + runs + 2 * runs - fisher_self.astype(jnp.int32) - mirror_self.astype(jnp.int32)

    def rows(h):
        return pl.ds(h * part, part)

    def chunk(way, i):
        if way == 0:
            return lax.rem(z + depth - 1 + ahead[0] - i, depth)
        return lax.rem(z + depth + 1 - ahead[1] + i, depth)

    def hop(way, i, p, src):
        e, h = pieces[p]
        return remote(
            src, ring.at[way, i, e, rows(h)], rs.at[way, i, p], rr.at[way, i, p], next_to(way))

    def first(way, p):
        e, h = pieces[p]
        own = lax.rem(z + depth + (ahead[0] if way == 0 else -ahead[1]), depth)
        return hop(way, 0, p, acc.at[2 * own + e, rows(h)])

    def later(way, i, p):
        e, h = pieces[p]
        return hop(way, i + 1, p, ring.at[way, i, e, rows(h)])

    def arrive(way, i, p):
        e, h = pieces[p]
        dst = ring.at[way, i, e, rows(h)]
        pltpu.make_async_copy(dst, dst, rr.at[way, i, p]).wait()

    def step(i, ways):
        for p, (e, h) in enumerate(pieces):
            for way in ways:
                arrive(way, i, p)
                ring[way, i, e, rows(h)] += acc[2 * chunk(way, i) + e, rows(h)]
                later(way, i, p).start()

    ways = [way for way in range(2) if ahead[way] > 0]
    both = max(0, ahead[1] - 1)
    def run(finish):
        def complete(b):
            for e in range(2):
                finish(2 * b + e)

        def start_of(way):
            return lax.rem(z + depth + (ahead[0] if way == 0 else -ahead[1]), depth)

        for way in ways:
            complete(start_of(way))
            for p in range(len(pieces)):
                first(way, p).start()
        def next_step(i, ways):
            for way in ways:
                complete(chunk(way, i))
            step(i, ways)

        loop(0, both, lambda i: next_step(i, [0, 1]))
        for i in range(both, ahead[0] - 1):
            next_step(i, [0])
        complete(z)
        for way in ways:
            for p in range(len(pieces)):
                arrive(way, ahead[way] - 1, p)
        for e in range(2):
            total = acc[2 * z + e]
            for way in ways:
                total += ring[way, ahead[way] - 1, e]
            slices = total.reshape(COUPLE, runs, BS // runs, BS)
            fin[:, e] = jnp.concatenate([slices[c] for c in range(COUPLE)], axis=1).astype(jnp.bfloat16)

        def out_f(t):
            return remote(fin.at[t], fbuf.at[pl.ds(2 * z, 2)], fs.at[t], fr.at[z], fisher_to(t))

        def out_m(e, t):
            return remote(fin.at[t, e], mbuf.at[plane], ms.at[e, t], mr.at[plane], mirror_to(e, t))

        def self_f():
            return pltpu.make_async_copy(fin.at[mine], fbuf.at[pl.ds(2 * z, 2)], fr.at[z])

        def self_m():
            return pltpu.make_async_copy(
                fin.at[mine, lax.rem(region, 2)], mbuf.at[plane], mr.at[plane])

        def is_self_m(e, t):
            return (2 * z + e == region) & (t == mine)

        def send(k):
            t = lax.rem(mine + k, runs)

            @pl.when(jnp.logical_not(fisher_self & (t == mine)))
            def _():
                out_f(t).start()

            for e in range(2):
                @pl.when(jnp.logical_not(is_self_m(e, t)))
                def _():
                    out_m(e, t).start()

        loop(0, runs, send)

        @pl.when(fisher_self)
        def _():
            self_f().start()

        @pl.when(mirror_self)
        def _():
            self_m().start()

        def got_f(k):
            dst = fbuf.at[pl.ds(2 * k, 2)]
            pltpu.make_async_copy(dst, dst, fr.at[k]).wait()

        def got_m(s):
            dst = mbuf.at[s]
            pltpu.make_async_copy(dst, dst, mr.at[s]).wait()

        loop(0, depth, got_f)
        loop(0, planes, got_m)

        for p in range(len(pieces)):
            for way in ways:
                first(way, p).wait_send()

        def sent(way, i):
            for p in range(len(pieces)):
                later(way, i, p).wait_send()

        for way in ways:
            loop(0, ahead[way] - 1, functools.partial(sent, way))

        def sent_out(t):
            @pl.when(jnp.logical_not(fisher_self & (t == mine)))
            def _():
                out_f(t).wait_send()

            for e in range(2):
                @pl.when(jnp.logical_not(is_self_m(e, t)))
                def _():
                    out_m(e, t).wait_send()

        loop(0, runs, sent_out)

    return greet_all, greeted, run


def fisher_kernel(
    sizes, shard, counts, table, fbuf, mbuf, acc, ring, fin, rs, rr, fs, fr, ms, mr,
    sens, ztab, xtab, stab, zs, zr, ys, yr, ps, pr, tzs, tzr, txs, txr, tsem, *bufs,
):
    masked, zbufs, tbufs, turned, outbufs, inbufs = (
        bufs[i * SPLIT:(i + 1) * SPLIT] for i in range(6))
    nx, nz, nh, ny, nc = sizes
    x, zlo = lax.axis_index("x"), lax.axis_index("zlo")
    y, core = lax.axis_index("y"), lax.axis_index("core")
    rho = y * nc + core
    plane = x * nz + rho
    planes = nx * nz
    stride = 11 % planes
    blocks = masked[0].shape[1]
    sub = [m.shape[2] for m in masked]
    offset = [sum(sub[:s]) for s in range(SPLIT)]
    first_run = (lax.axis_index("zhi") * nz + rho) * (sens.shape[0] // OBS)

    def z_at(d):
        return {"zlo": lax.rem(zlo + d, nz)}

    def yc_at(t):
        return {"y": t // nc, "core": lax.rem(t, nc)}

    def x_at(d):
        return {"x": lax.rem(x + d, nx)}

    def plane_at(t):
        r = lax.rem(t, nz)
        return {"x": t // nz, "y": r // nc, "core": lax.rem(r, nc)}

    barrier = pltpu.get_barrier_semaphore()
    greet_all, greeted, reduce_over_z = reduction(
        sizes, barrier, acc, fbuf, mbuf, ring, fin, rs, rr, fs, fr, ms, mr)
    load = pltpu.make_async_copy(shard, sens, tsem)
    load.start()
    greet_all()
    loop(1, nz, lambda d: pl.semaphore_signal(barrier, inc=1, device_id=z_at(d), device_id_type=MESH))
    loop(1, planes, lambda g: pl.semaphore_signal(
        barrier, inc=1, device_id=plane_at(lax.rem(plane + g, planes)), device_id_type=MESH))

    def table_copy(d):
        return remote(table, ztab.at[zlo], tzs.at[d], tzr.at[d], z_at(d))

    def row_copy(x_from, d):
        return remote(ztab, xtab.at[x_from], txs.at[d], txr.at[d], x_at(d))

    def z_copy(s, d):
        return remote(
            masked[s].at[lax.rem(zlo + d, nz)], zbufs[s].at[zlo], zs.at[s, d], zr.at[s, d], z_at(d))

    def y_copy(s, e):
        t = lax.rem(rho + e, nz)
        return remote(zbufs[s].at[t], tbufs[s].at[:, rho], ys.at[s, e], yr.at[s, e], yc_at(t))

    def p_copy(s, g):
        return remote(
            outbufs[s].at[g], inbufs[s].at[plane], ps.at[s, g], pr.at[s, g],
            plane_at(lax.rem(plane + g, planes)))

    def mask(j, s):
        start = pl.multiple_of(j * sum(sub) + offset[s], sub[-1])
        run = (start + lax.broadcasted_iota(jnp.int32, (sub[s], BS), 0)) // OBS + first_run
        for b in range(blocks):
            value = sens[pl.ds(start, sub[s]), b * BS:(b + 1) * BS].astype(jnp.float32)
            masked[s][j, b] = jnp.where(run < counts[b], value, 0.0).astype(jnp.bfloat16)

    early = min(nz // 2, nz - 1)

    def z_self(s):
        mask(zlo, s)
        pltpu.make_async_copy(masked[s].at[zlo], zbufs[s].at[zlo], zr.at[s, 0]).start()

    def z_one(s, i):
        d = lax.rem(i * 3, nz)
        mask(lax.rem(zlo + d, nz), s)
        z_copy(s, d).start()

    def z_wait(s, d):
        dst = zbufs[s].at[lax.rem(zlo + nz - d, nz)]
        pltpu.make_async_copy(dst, dst, zr.at[s, d]).wait()

    def relay(s):
        def one(i):
            d = lax.rem(i * 3, nz)
            z_wait(s, d)
            e = lax.rem(zlo + 2 * nz - d - rho, nz)

            @pl.when(e == 0)
            def _():
                pltpu.make_async_copy(zbufs[s].at[rho], tbufs[s].at[:, rho], yr.at[s, 0]).start()

            @pl.when(e > 0)
            def _():
                y_copy(s, e).start()

        if s + 1 < SPLIT:
            def both(i):
                one(i)
                z_one(s + 1, i + 1)

            loop(0, early, both)
            loop(early, nz, one)
            z_self(s + 1)
        else:
            loop(0, nz, one)

    def block(s, b):
        return tbufs[s][b].reshape(nz * sub[s], BS)

    def asked(t):
        return stab[t // nz, lax.rem(t, nz), 0, plane]

    def pick(s):
        def ready(e):
            dst = tbufs[s].at[:, lax.rem(rho + nz - e, nz)]
            pltpu.make_async_copy(dst, dst, yr.at[s, e]).wait()

        loop(0, nz, ready)

        def one(i):
            g = lax.rem(i * stride, planes)
            outbufs[s][g] = block(s, asked(lax.rem(plane + g, planes)))
            p_copy(s, g).start()

        groups = nz - 1 - early if s + 1 < SPLIT else 0
        begin = 1
        for j in range(groups):
            end = 1 + (planes - 1) * (j + 1) // (groups + 1)
            loop(begin, end, one)
            z_one(s + 1, early + 1 + j)
            begin = end
        loop(begin, planes, one)
        inbufs[s][plane] = block(s, asked(plane))

    def turn(s):
        def one(b):
            turned[s][b] = tbufs[s][b].reshape(nz * sub[s], BS).T

        loop(0, blocks, one)

    def product(s, q):
        g = lax.rem(plane + planes - q, planes)

        @pl.when(g > 0)
        def _():
            dst = inbufs[s].at[q]
            pltpu.make_async_copy(dst, dst, pr.at[s, g]).wait()

        near = jnp.concatenate(
            [turned[s][stab[x, rho, 1 + c, q]] for c in range(COUPLE)], axis=0)
        value = jnp.dot(near, inbufs[s][q], preferred_element_type=jnp.float32)
        if s == 0:
            acc[q] = value
        else:
            acc[q] += value

    def multiply(s):
        def one(i):
            g = lax.rem(i * stride, planes)
            product(s, lax.rem(plane + planes - g, planes))

        loop(0, planes, one)

    load.wait()
    pl.semaphore_wait(barrier, nz - 1 + planes - 1 + greeted)

    pltpu.make_async_copy(table, ztab.at[zlo], tzr.at[0]).start()
    loop(1, nz, lambda d: table_copy(d).start())
    loop(1, nz, lambda i: z_one(0, i))
    z_self(0)

    def table_wait(d):
        dst = ztab.at[lax.rem(zlo + nz - d, nz)]
        pltpu.make_async_copy(dst, dst, tzr.at[d]).wait()

    loop(0, nz, table_wait)
    pltpu.make_async_copy(ztab, xtab.at[x], txr.at[0]).start()
    loop(1, nx, lambda d: row_copy(x, d).start())

    for s in range(SPLIT):
        relay(s)
        if s == 0:
            def row_wait(d):
                dst = xtab.at[lax.rem(x + nx - d, nx)]
                pltpu.make_async_copy(dst, dst, txr.at[d]).wait()

            loop(0, nx, row_wait)
            fetch = pltpu.make_async_copy(xtab, stab, tsem)
            fetch.start()
            fetch.wait()
        pick(s)
        if s > 0:
            multiply(s - 1)
        turn(s)
    reduce_over_z(functools.partial(product, SPLIT - 1))

    loop(1, nz, lambda d: table_copy(d).wait_send())
    loop(1, nx, lambda d: row_copy(x, d).wait_send())
    for s in range(SPLIT):
        loop(1, nz, lambda d: z_copy(s, d).wait_send())
        loop(1, nz, lambda e: y_copy(s, e).wait_send())
        loop(1, planes, lambda g: p_copy(s, g).wait_send())


def shards(sensitivity, run_counts, req_owner, req_block, coupled):
    rows_dev, cols = sensitivity.shape
    blocks = run_counts.shape[0]
    nx, nz, nh, ny, nc = (lax.axis_size(a) for a in ("x", "zlo", "zhi", "y", "core"))
    regions = nx * nz
    runs = nh * ny * nc
    sub = [n * rows_dev // (nz * sum(PARTS)) for n in PARTS]
    vmem = pl.BlockSpec(memory_space=pltpu.VMEM)
    dma = pltpu.SemaphoreType.DMA

    fields = jnp.concatenate([req_block[:, None], coupled], axis=1)
    hit = req_owner[:, 0][:, None] == jnp.arange(regions, dtype=jnp.int32)[None, :]
    sorted_fields = jnp.sum(jnp.where(hit[:, None, :], fields[:, :, None], 0), axis=0)
    table = jnp.pad(sorted_fields, ((0, 8 - 1 - COUPLE), (0, 128 - regions)))

    share = BS // runs
    depth = nh * nz
    by_owner, by_source = pl.pallas_call(
        functools.partial(fisher_kernel, (nx, nz, nh, ny, nc)),
        out_shape=[jax.ShapeDtypeStruct((regions, COUPLE * share, BS), jnp.bfloat16)] * 2,
        in_specs=[pl.BlockSpec(memory_space=pl.ANY), pl.BlockSpec(memory_space=pltpu.SMEM), vmem],
        out_specs=[vmem, vmem],
        scratch_shapes=[
            pltpu.VMEM((regions, COUPLE * BS, BS), jnp.float32),
            pltpu.VMEM((2, depth // 2, 2, COUPLE * BS, BS), jnp.float32),
            pltpu.VMEM((runs, 2, COUPLE * share, BS), jnp.bfloat16),
            dma((2, depth // 2, PIECES)), dma((2, depth // 2, PIECES)),
            dma((runs,)), dma((depth,)),
            dma((2, runs)), dma((regions,)),
            pltpu.VMEM((rows_dev, cols), jnp.bfloat16),
            pltpu.VMEM((nz, 8, 128), jnp.int32),
            pltpu.VMEM((nx, nz, 8, 128), jnp.int32),
            pltpu.SMEM((nx, nz, 8, 128), jnp.int32),
            dma((SPLIT, nz)), dma((SPLIT, nz)),
            dma((SPLIT, nz)), dma((SPLIT, nz)),
            dma((SPLIT, regions)), dma((SPLIT, regions)),
            dma((nz,)), dma((nz,)), dma((nx,)), dma((nx,)), dma,
        ] + [
            pltpu.VMEM(shape, jnp.bfloat16)
            for shape in (
                [(nz, blocks, n, BS) for n in sub] * 2
                + [(blocks, nz, n, BS) for n in sub]
                + [(blocks, BS, nz * n) for n in sub]
                + [(regions, nz * n, BS) for n in sub] * 2)
        ],
        compiler_params=pltpu.CompilerParams(
            collective_id=0, has_side_effects=True, vmem_limit_bytes=54 << 20),
    )(sensitivity, run_counts, table)

    fisher = jnp.take(by_owner, req_owner[:, 0], axis=0).reshape(-1, COUPLE, share, BS)
    mirror = jnp.swapaxes(by_source.reshape(-1, COUPLE, share, BS), 2, 3)
    return fisher, mirror.reshape(1, regions, 1, COUPLE, BS, share)


def solution(mesh):
    fine = Mesh(mesh.devices.reshape(4, 8, 2, 4, 2), ("x", "zlo", "zhi", "y", "core"))
    return build(fine)


def build(fine):
    in_specs = (P(RUN, REGION), P(REGION), P(REGION, None), P(REGION), P(REGION, None))
    out_specs = (P(REGION, None, RUN, None), P(REGION, None, None, None, None, RUN))
    return jax.shard_map(shards, mesh=fine, in_specs=in_specs, out_specs=out_specs, check_vma=False)
```
